32 devices in a mesh: dp: 8 (over y, x, core), tok: 4 (over z).
Axes of the slice: x: 2, y: 2, z: 4, core: 2. Of those that a mesh axis runs over, the one named last changes fastest.
Arguments:
- inputs: bfloat16 [4, 256, 2048], P('tok', 'dp'), may hold values from -6 to 6
- cotangent: bfloat16 [4, 256, 2048], P('tok', 'dp'), may hold values from -6 to 6
- norm_gain: float32 [4, 2048], P('tok'), may hold values from 0.5 to 1.5
- router_weight: bfloat16 [4, 2048, 4], P('tok'), may hold values from -0.125 to 0.125
- route_ids: int32 [4, 256, 2], P('tok'), may hold values from 0 to 3, all different within a row; in each aligned block of 256 rows (0 to 255, 256 to 511, ..., all dimensions but the last counted through in order) at most 160 rows name the same one
- w_gate: bfloat16 [4, 4, 2048, 4096], P('tok', None, None, 'dp'), may hold values from -0.125 to 0.125
- w_up: bfloat16 [4, 4, 2048, 4096], P('tok', None, None, 'dp'), may hold values from -0.125 to 0.125
- w_down: bfloat16 [4, 4, 4096, 2048], P('tok', None, 'dp'), may hold values from -0.09375 to 0.09375
Outputs:
- grad_inputs: bfloat16 [4, 256, 2048], P('tok', 'dp')
- grad_gate: bfloat16 [4, 4, 2048, 4096], P('tok', None, None, 'dp')
- grad_up: bfloat16 [4, 4, 2048, 4096], P('tok', None, None, 'dp')
- grad_down: bfloat16 [4, 4, 4096, 2048], P('tok', None, 'dp')
- grad_router: float32 [4, 2048, 4], P('tok')
- grad_gain: float32 [4, 2048], P('tok')
The draws below stay inside these ranges and needn't reach their ends.
Inputs may be any that keep to these rules, and one draw needn't show every extreme that they name: `route_ids`: for each token the two experts of a sample differ; each expert of a token is chosen by at most 160 of its samples, a bound that some block reaches.
All inputs are finite; a program needn't handle non-finite values.
Results may differ from the reference program's by a relative error of at most 0.0095.
Values may be sent and summed in bfloat16 or wider, within the bound.
No kernel may reach another device: no remote copies, remote signals or barrier semaphores. Data moves between devices by JAX's collectives and lax.ppermute only.
A program may use at most 192 MiB of HBM per device.

```python
import math
import jax
import jax.numpy as jnp
import numpy as np
from jax import lax

D = 2048
H = 4096
EXP = 4
TOP = 2
TOKENS = 4
B = 256
CAP = 160
N_DP = 8


def levels(stream_key, extent, pieces, low, largest):
    level = 1.0
    for dim, blocks in pieces:
        draws = jax.random.uniform(jax.random.fold_in(jax.random.fold_in(stream_key, 6), dim), (blocks,), jnp.float32, low / len(pieces), largest / len(pieces))
        level = level * jnp.repeat(jnp.exp(draws), extent[dim] // blocks).reshape((-1,) + (1,) * (len(extent) - 1 - dim))
    return level


def shared_out(rng, own, number, rows, amount, top, reach, lean):
    ranking = jax.random.permutation(rng, amount)
    packed, usual = shares(amount, rows * top, reach, lean, True), shares(amount, rows * top, reach, lean, False)
    places = jnp.arange(amount)

    def named(lengths, offset_by):
        used = int((lengths > 0).sum())
        fixed = max(1, used // 4)
        shifted = fixed + (places - fixed + offset_by * (used - fixed)) % max(1, amount - fixed)
        return jnp.zeros((amount,), jnp.int32).at[ranking[jnp.where(places < fixed, places, shifted)]].set(jnp.asarray(lengths, jnp.int32))

    lengths = jnp.where(number % 4 == 0, named(packed, number // 4), named(usual, number - number // 4 - 1))
    mixed = jax.random.permutation(jax.random.fold_in(own, 3), amount)
    giver, taker = mixed[0:amount // 2 * 2:2], mixed[1:amount // 2 * 2:2]
    margin = jnp.minimum(lengths[giver] - 1, reach - lengths[taker]) // 2
    margin = jnp.where((giver == ranking[0]) | (taker == ranking[0]) | (lengths[taker] == 0), 0, jnp.maximum(margin, 0))
    shifted = jax.random.randint(jax.random.fold_in(own, 4), (amount // 2,), 0, 1 << 20) % (margin + 1)
    lengths = lengths.at[giver].add(-shifted).at[taker].add(shifted)
    labels = jnp.searchsorted(jnp.cumsum(lengths), jnp.arange(rows * top), side="right").astype(jnp.int32)
    grid = labels.reshape(top, rows).T
    grid = grid[jax.random.permutation(jax.random.fold_in(own, 1), rows)]
    offset_by = jax.random.randint(jax.random.fold_in(own, 2), (rows, 1), 0, top)
    return jnp.take_along_axis(grid, (jnp.arange(top)[None, :] + offset_by) % top, axis=1)


def shares(count, total, limit, skew, full):
    portions = [(1 << 20) // math.isqrt(grade ** skew) + 1 for grade in range(1, count + 1)]
    largest = limit if full else min(limit, max(-(-total // count), total * portions[0] // sum(portions)))
    least = 1 if total - largest >= count - 1 else 0
    holding, rest = [largest] + [least] * (count - 1), total - largest - least * (count - 1)
    while rest > 0:
        free = [i for i in range(1, count) if holding[i] < largest] or [i for i in range(1, count) if holding[i] < limit]
        mass, remaining = sum([portions[i] for i in free]), rest
        for i in free:
            more = min(limit - holding[i], max(1, remaining * portions[i] // mass), rest)
            holding[i] = holding[i] + more
            rest = rest - more
    return np.array(holding)


def centred(own_key, shape, spread, limit, shards=(), held_as=jnp.bfloat16):
    factor_of = levels(own_key, shape, shards, -0.22, 0.18) if shards else 1.0
    entries = jax.random.normal(own_key, shape, jnp.float32) * spread * factor_of
    return jnp.minimum(jnp.maximum(entries, -limit), limit).astype(held_as)


def setup_inputs(seed: int = 0) -> dict:
    splits = jax.random.split(jax.random.key(seed), 9)
    inputs = centred(splits[0], (TOKENS, B, D), 1.0, 6.0, ((0, 4), (1, 8)))
    cotangent = centred(splits[1], (TOKENS, B, D), 1.0, 6.0, ((0, 4), (1, 8)))
    norm_gain = jnp.clip(1.0 + 0.1 * jax.random.normal(splits[2], (TOKENS, D), jnp.float32), 0.5, 1.5)
    router_weight = centred(splits[3], (TOKENS, D, EXP), D ** -0.5, 0.125, ((0, 4),))
    route_ids_keys = jax.random.split(jax.random.fold_in(splits[4], 1), TOKENS * B // B)
    route_ids_turns = jax.random.permutation(jax.random.fold_in(splits[4], 3), TOKENS * B // B)
    route_ids = jax.vmap(lambda own, number: shared_out(jax.random.fold_in(splits[4], 2), own, number, B, EXP, TOP, CAP, 1))(route_ids_keys, route_ids_turns).reshape((TOKENS, B, TOP))
    w_gate = centred(splits[5], (TOKENS, EXP, D, H), D ** -0.5, 0.125, ((0, 4), (3, 8)))
    w_up = centred(splits[6], (TOKENS, EXP, D, H), D ** -0.5, 0.125, ((0, 4), (3, 8)))
    w_down = centred(splits[7], (TOKENS, EXP, H, D), H ** -0.5, 0.09375, ((0, 4), (2, 8)))
    return dict(inputs=inputs, cotangent=cotangent, norm_gain=norm_gain, router_weight=router_weight, route_ids=route_ids, w_gate=w_gate, w_up=w_up, w_down=w_down)


def slot_table(route_row, expert, capacity):
    flat_routes = route_row.reshape(-1)
    hit_mask = (flat_routes == expert).astype(jnp.int32)
    where_to = jnp.where(hit_mask > 0, jnp.cumsum(hit_mask) - 1, capacity).astype(jnp.int32)
    pair_ids = jnp.arange(flat_routes.shape[0], dtype=jnp.int32)
    chosen = jnp.zeros((capacity + 1,), jnp.int32).at[where_to].set(pair_ids)[:capacity]
    filled = jnp.zeros((capacity + 1,), jnp.float32).at[where_to].set(1.0)[:capacity]
    return (chosen, filled)

def expert_backward(sample_rows, cot_rows, slot_gate, gate_mat, up_mat, down_mat):
    pre_gate = jnp.dot(sample_rows, gate_mat, preferred_element_type=jnp.float32)
    pre_up = jnp.dot(sample_rows, up_mat, preferred_element_type=jnp.float32)
    sigma_gate = jax.nn.sigmoid(pre_gate)
    silu_gate = pre_gate * sigma_gate
    activation = (silu_gate * pre_up).astype(jnp.bfloat16)
    back_hidden = jnp.dot(cot_rows, down_mat.T, preferred_element_type=jnp.float32)
    gate_share = lax.optimization_barrier(jnp.sum(activation.astype(jnp.float32) * back_hidden, axis=1))
    scaled_back = slot_gate[:, None] * back_hidden
    grad_pre_gate = (scaled_back * pre_up * sigma_gate * (1.0 + pre_gate * (1.0 - sigma_gate))).astype(jnp.bfloat16)
    grad_pre_up = (scaled_back * silu_gate).astype(jnp.bfloat16)
    scaled_cot = (slot_gate[:, None] * cot_rows.astype(jnp.float32)).astype(jnp.bfloat16)
    gate_grad = jnp.dot(sample_rows.T, grad_pre_gate, preferred_element_type=jnp.float32)
    up_grad = jnp.dot(sample_rows.T, grad_pre_up, preferred_element_type=jnp.float32)
    down_grad = jnp.dot(activation.T, scaled_cot, preferred_element_type=jnp.float32)
    return (gate_share, gate_grad, up_grad, down_grad, grad_pre_gate, grad_pre_up)

def run_parts(grad_pre, weight_mat):
    slots, hidden = grad_pre.shape
    width = weight_mat.shape[0]
    grad_view = grad_pre.astype(jnp.float32).reshape(slots, N_DP, hidden // N_DP)
    weight_view = weight_mat.astype(jnp.float32).reshape(width, N_DP, hidden // N_DP)
    return jnp.einsum('cph,dph->pcd', grad_view, weight_view)

def reference(inputs, cotangent, norm_gain, router_weight, route_ids, w_gate, w_up, w_down):
    num_tokens, all_rows, feat_width = inputs.shape
    head_width = feat_width // num_tokens
    heads_view = inputs.reshape(num_tokens, all_rows, num_tokens, head_width)
    mixed = jnp.transpose(heads_view, (2, 1, 0, 3)).reshape(inputs.shape)
    summed = inputs.astype(jnp.float32) + mixed.astype(jnp.float32)
    inv_rms = lax.rsqrt(lax.optimization_barrier(jnp.mean(summed * summed, axis=2, keepdims=True)) + 1e-06)
    normed = (summed * inv_rms * norm_gain[:, None, :]).astype(jnp.bfloat16)
    expert_ids = jnp.arange(EXP, dtype=jnp.int32)
    grad_summed_list, gate_list, up_list, down_list, router_list, gain_list = ([], [], [], [], [], [])
    for token_id in range(num_tokens):
        token_rows = normed[token_id]
        token_cot = cotangent[token_id]
        token_routes = route_ids[token_id]
        logits = jnp.dot(token_rows, router_weight[token_id], preferred_element_type=jnp.float32)
        gate_prob = jax.nn.sigmoid(jnp.take_along_axis(logits, token_routes, axis=1))
        gate_flat = gate_prob.reshape(-1)
        share_sum = jnp.zeros((all_rows * TOP,), jnp.float32)
        part_sums = jnp.zeros((N_DP, all_rows, feat_width), jnp.float32)
        gates, ups, downs = ([], [], [])
        for expert in range(EXP):
            chosen, filled = slot_table(token_routes, expert, CAP)
            row_ids = chosen // TOP
            slot_gate = gate_flat[chosen] * filled
            gate_share, gate_grad, up_grad, down_grad, grad_pre_gate, grad_pre_up = expert_backward(token_rows[row_ids], token_cot[row_ids], slot_gate, w_gate[token_id, expert], w_up[token_id, expert], w_down[token_id, expert])
            part_rows = run_parts(grad_pre_gate, w_gate[token_id, expert]) + run_parts(grad_pre_up, w_up[token_id, expert])
            part_sums = part_sums.at[:, row_ids].add(part_rows)
            share_sum = share_sum.at[chosen].add(gate_share * filled)
            gates.append(gate_grad.astype(jnp.bfloat16))
            ups.append(up_grad.astype(jnp.bfloat16))
            downs.append(down_grad.astype(jnp.bfloat16))
        rounded_parts = lax.optimization_barrier(part_sums.astype(jnp.bfloat16))
        expert_grad = lax.optimization_barrier(jnp.sum(rounded_parts.astype(jnp.float32), axis=0))
        logit_grad = share_sum.reshape(all_rows, TOP) * gate_prob * (1.0 - gate_prob)
        picked = (token_routes[:, :, None] == expert_ids[None, None, :]).astype(jnp.float32)
        router_coef = lax.optimization_barrier(jnp.sum(logit_grad[:, :, None] * picked, axis=1))
        router_list.append(jnp.dot(token_rows.astype(jnp.float32).T, router_coef, precision=lax.Precision.HIGHEST))
        grad_normed = expert_grad + jnp.dot(router_coef, router_weight[token_id].astype(jnp.float32).T, precision=lax.Precision.HIGHEST)
        token_sum = summed[token_id]
        token_inv = inv_rms[token_id]
        gain_list.append(lax.optimization_barrier(jnp.sum(grad_normed * token_sum * token_inv, axis=0)))
        scaled_grad = grad_normed * norm_gain[token_id][None, :]
        grad_summed = token_inv * scaled_grad - token_sum * token_inv ** 3 * lax.optimization_barrier(jnp.mean(scaled_grad * token_sum, axis=1, keepdims=True))
        grad_summed_list.append(grad_summed + token_cot.astype(jnp.float32))
        gate_list.append(jnp.stack(gates))
        up_list.append(jnp.stack(ups))
        down_list.append(jnp.stack(downs))
    grad_summed = jnp.stack(grad_summed_list)
    grad_view = grad_summed.reshape(num_tokens, all_rows, num_tokens, head_width)
    grad_inputs = (grad_summed + jnp.transpose(grad_view, (2, 1, 0, 3)).reshape(grad_summed.shape)).astype(jnp.bfloat16)
    return (grad_inputs, jnp.stack(gate_list), jnp.stack(up_list), jnp.stack(down_list), jnp.stack(router_list), jnp.stack(gain_list))
```

```python
import functools

import jax
import jax.numpy as jnp
from jax import lax
from jax.experimental import pallas as pl
from jax.experimental.pallas import tpu as pltpu
from jax.sharding import PartitionSpec as P

BF16 = jnp.bfloat16
F32 = jnp.float32
MIB = 1024 * 1024


def dot(left, right, dims):
    return lax.dot_general(left, right, (dims, ((), ())), preferred_element_type=F32)


NN = ((1,), (0,))
NT = ((1,), (1,))
TN = ((0,), (0,))


def exchange(value, axis, distance):
    size = lax.axis_size(axis)
    return lax.ppermute(value, axis, [(i, i ^ distance) for i in range(size)])


def gather_chunks(rows):
    size = lax.axis_size("dp")
    chunks = [rows] + [None] * (size - 1)
    for s in range(2, size, 2):
        chunks[s] = exchange(rows, "dp", s)
    for s in range(1, size, 2):
        chunks[s] = exchange(chunks[s - 1], "dp", 1)
    return chunks


def head_slice(slot, width):
    return pl.ds(pl.multiple_of(slot * width, width), width)


def norm_kernel(num_tokens, *refs):
    x_ref, gain_ref = refs[:2]
    heads = refs[2 : 1 + num_tokens]
    normed_ref, summed_ref, mixed = refs[1 + num_tokens :]
    me = lax.axis_index("tok")
    width = x_ref.shape[2] // num_tokens
    own = head_slice(me, width)
    mixed[:, own] = x_ref[0, :, own].astype(F32)
    for s in range(1, num_tokens):
        mixed[:, head_slice(me ^ s, width)] = heads[s - 1][...].astype(F32)
    summed = x_ref[0].astype(F32) + mixed[...]
    inv_rms = lax.rsqrt(jnp.mean(summed * summed, axis=1, keepdims=True) + 1e-06)
    normed_ref[...] = (summed * inv_rms * gain_ref[...]).astype(BF16)
    summed_ref[...] = summed


def norm_rows(x, gain, heads):
    _, rows, width = x.shape
    num_tokens = lax.axis_size("tok")
    return pl.pallas_call(
        functools.partial(norm_kernel, num_tokens),
        out_shape=(
            jax.ShapeDtypeStruct((rows, width), BF16),
            jax.ShapeDtypeStruct((rows, width), F32),
        ),
        scratch_shapes=[pltpu.VMEM((rows, width), F32)],
        name="norm_rows",
    )(x, gain, *heads)


def back_kernel(size, *refs):
    chunks, (down_ref, back_ref, cot) = refs[:size], refs[size:]
    own = chunks[0].shape[0]

    @pl.when(pl.program_id(0) == 0)
    def _():
        for s in range(size):
            cot[s * own : (s + 1) * own] = chunks[s][...]

    back_ref[0] = dot(cot[...], down_ref[0, 0], NT)


def back_hidden(chunks, w_down):
    size = len(chunks)
    own, width = chunks[0].shape
    _, experts, hidden, _ = w_down.shape
    rows = size * own
    chunk_spec = pl.BlockSpec((own, width), lambda e: (0, 0))
    return pl.pallas_call(
        functools.partial(back_kernel, size),
        grid=(experts,),
        in_specs=[chunk_spec] * size
        + [pl.BlockSpec((1, 1, hidden, width), lambda e: (0, e, 0, 0))],
        out_specs=pl.BlockSpec((1, rows, hidden), lambda e: (e, 0, 0)),
        out_shape=jax.ShapeDtypeStruct((experts, rows, hidden), F32),
        scratch_shapes=[pltpu.VMEM((rows, width), BF16)],
        compiler_params=pltpu.CompilerParams(vmem_limit_bytes=24 * MIB),
        cost_estimate=pl.CostEstimate(
            flops=2 * experts * rows * hidden * width,
            bytes_accessed=experts * hidden * (width * 2 + rows * 4) + rows * width * 2,
            transcendentals=0,
        ),
        name="back_hidden",
    )(*chunks, w_down)


def expert_kernel(size, *refs):
    chunks = refs[:size]
    (gate_ref, up_ref, back_ref, route_ref, router_ref, gain_ref) = refs[size : size + 6]
    (pre_gate_out, pre_up_out, act_out, kept_out, sent_out, small_out) = refs[size + 6 : size + 12]
    normed, total, prob, share = refs[size + 12 :]
    own, width = chunks[0].shape
    experts = router_ref.shape[0]
    expert = pl.program_id(0)
    rows = size * own
    lanes = lax.broadcasted_iota(jnp.int32, (rows, experts), 1)

    @pl.when(expert == 0)
    def _():
        me = lax.axis_index("dp")
        for s in range(size):
            here = slice(s * own, (s + 1) * own)
            normed[here] = chunks[s][...]
            routes = route_ref[0, pl.ds(pl.multiple_of((me ^ s) * own, own), own), :]
            ids = lanes[here]
            hit = (routes[:, 0:1] == ids) | (routes[:, 1:2] == ids)
            for k in range(2, route_ref.shape[2]):
                hit = hit | (routes[:, k : k + 1] == ids)
            share[here] = hit.astype(F32)
        prob[...] = jax.nn.sigmoid(dot(normed[...], router_ref[...], NT))

    mine = (lanes == expert).astype(F32)
    gate = jnp.sum(mine * prob[...] * share[...], axis=1, keepdims=True)
    pre_gate = dot(normed[...], gate_ref[0, 0], NN)
    pre_up = dot(normed[...], up_ref[0, 0], NN)
    back = back_ref[0]
    sigma = jax.nn.sigmoid(pre_gate)
    silu = pre_gate * sigma
    act = silu * pre_up
    own_share = jnp.sum(act * back, axis=1, keepdims=True)
    share[...] = jnp.where(lanes == expert, share[...] * own_share, share[...])
    scaled = gate * back
    grad_gate = (scaled * pre_up * (sigma * (1.0 + pre_gate * (1.0 - sigma)))).astype(BF16)
    grad_up = (scaled * silu).astype(BF16)
    pre_gate_out[0] = grad_gate
    pre_up_out[0] = grad_up
    act_out[0] = (gate * act).astype(BF16)
    part = dot(grad_gate, gate_ref[0, 0], NT) + dot(grad_up, up_ref[0, 0], NT)

    @pl.when(expert == 0)
    def _():
        total[...] = part

    @pl.when(expert > 0)
    def _():
        total[...] += part

    @pl.when(expert == experts - 1)
    def _():
        coef = share[...] * prob[...] * (1.0 - prob[...])
        high = coef.astype(BF16)
        rest = coef - high.astype(F32)
        middle = rest.astype(BF16)
        low = (rest - middle.astype(F32)).astype(BF16)
        router = router_ref[...]
        grad = total[...]
        small = jnp.zeros((experts, width), F32)
        for term in (low, middle, high):
            grad = grad + dot(term, router, NN)
            small = small + dot(term, normed[...], TN)
        small_out[:experts] = small
        gain = jnp.sum(grad * normed[...].astype(F32), axis=0, keepdims=True) / gain_ref[...]
        small_out[experts:] = jnp.broadcast_to(gain, (8 - experts, width))
        for s in range(size):
            target = sent_out if s % 2 else kept_out
            target[s // 2] = grad[s * own : (s + 1) * own].astype(BF16)


def experts_backward(chunks, w_gate, w_up, back, route_ids, router_rows, gain):
    size = len(chunks)
    own, width = chunks[0].shape
    _, experts, _, hidden = w_gate.shape
    rows = size * own
    whole = lambda a: pl.BlockSpec(a.shape, lambda e: (0,) * a.ndim)
    weight = pl.BlockSpec((1, 1, width, hidden), lambda e: (0, e, 0, 0))
    per_expert = pl.BlockSpec((1, rows, hidden), lambda e: (e, 0, 0))
    half = jax.ShapeDtypeStruct((size // 2, own, width), BF16)
    small = jax.ShapeDtypeStruct((8, width), F32)
    hidden_out = jax.ShapeDtypeStruct((experts, rows, hidden), BF16)
    return pl.pallas_call(
        functools.partial(expert_kernel, size),
        grid=(experts,),
        in_specs=[whole(c) for c in chunks]
        + [weight, weight, per_expert, whole(route_ids), whole(router_rows), whole(gain)],
        out_specs=(per_expert, per_expert, per_expert, whole(half), whole(half), whole(small)),
        out_shape=(hidden_out, hidden_out, hidden_out, half, half, small),
        scratch_shapes=[
            pltpu.VMEM((rows, width), BF16),
            pltpu.VMEM((rows, width), F32),
            pltpu.VMEM((rows, experts), F32),
            pltpu.VMEM((rows, experts), F32),
        ],
        compiler_params=pltpu.CompilerParams(vmem_limit_bytes=48 * MIB),
        cost_estimate=pl.CostEstimate(
            flops=8 * experts * rows * hidden * width,
            bytes_accessed=experts * hidden * (width * 4 + rows * 10) + rows * width * 4,
            transcendentals=experts * rows * hidden,
        ),
        name="experts_backward",
    )(*chunks, w_gate, w_up, back, route_ids, router_rows, gain)


def weight_kernel(size, *refs):
    normed_chunks, cot_chunks = refs[:size], refs[size : 2 * size]
    pre_gate_ref, pre_up_ref, act_ref, gate_out, up_out, down_out, normed, cot = refs[2 * size :]
    own = normed_chunks[0].shape[0]

    @pl.when(pl.program_id(0) == 0)
    def _():
        for s in range(size):
            here = slice(s * own, (s + 1) * own)
            normed[here] = normed_chunks[s][...]
            cot[here] = cot_chunks[s][...]

    gate_out[0, 0] = dot(normed[...], pre_gate_ref[0], TN).astype(BF16)
    up_out[0, 0] = dot(normed[...], pre_up_ref[0], TN).astype(BF16)
    down_out[0, 0] = dot(act_ref[0], cot[...], TN).astype(BF16)


def weight_gradients(normed_chunks, cot_chunks, pre_gate, pre_up, act):
    size = len(normed_chunks)
    own, width = normed_chunks[0].shape
    experts, rows, hidden = act.shape
    chunk_spec = pl.BlockSpec((own, width), lambda e: (0, 0))
    per_expert = pl.BlockSpec((1, rows, hidden), lambda e: (e, 0, 0))
    wide = pl.BlockSpec((1, 1, width, hidden), lambda e: (0, e, 0, 0))
    return pl.pallas_call(
        functools.partial(weight_kernel, size),
        grid=(experts,),
        in_specs=[chunk_spec] * (2 * size) + [per_expert] * 3,
        out_specs=(wide, wide, pl.BlockSpec((1, 1, hidden, width), lambda e: (0, e, 0, 0))),
        out_shape=(
            jax.ShapeDtypeStruct((1, experts, width, hidden), BF16),
            jax.ShapeDtypeStruct((1, experts, width, hidden), BF16),
            jax.ShapeDtypeStruct((1, experts, hidden, width), BF16),
        ),
        scratch_shapes=[pltpu.VMEM((rows, width), BF16)] * 2,
        compiler_params=pltpu.CompilerParams(vmem_limit_bytes=48 * MIB),
        cost_estimate=pl.CostEstimate(
            flops=6 * experts * rows * hidden * width,
            bytes_accessed=experts * hidden * (width * 6 + rows * 6) + rows * width * 4,
            transcendentals=0,
        ),
        name="weight_gradients",
    )(*normed_chunks, *cot_chunks, pre_gate, pre_up, act)


def norm_back_kernel(num_tokens, parts, *refs):
    sums, (summed_ref, gain_ref, cot_ref), outs = refs[:parts], refs[parts : parts + 3], refs[parts + 3 :]
    grad_ref, heads = outs[0], outs[1:]
    me = lax.axis_index("tok")
    grad_normed = sums[0][...].astype(F32)
    for s in sums[1:]:
        grad_normed = grad_normed + s[...].astype(F32)
    summed = summed_ref[...]
    inv_rms = lax.rsqrt(jnp.mean(summed * summed, axis=1, keepdims=True) + 1e-06)
    scaled = grad_normed * gain_ref[...]
    centre = jnp.mean(scaled * summed, axis=1, keepdims=True)
    grad = inv_rms * scaled - summed * (inv_rms * inv_rms * inv_rms * centre)
    grad_ref[...] = grad + cot_ref[0].astype(F32)
    width = summed.shape[1] // num_tokens
    for s in range(1, num_tokens):
        heads[s - 1][...] = grad_ref[:, head_slice(me ^ s, width)].astype(BF16)


def norm_backward(sums, summed, gain, cotangent):
    rows, width = summed.shape
    num_tokens = lax.axis_size("tok")
    head = jax.ShapeDtypeStruct((rows, width // num_tokens), BF16)
    return pl.pallas_call(
        functools.partial(norm_back_kernel, num_tokens, len(sums)),
        out_shape=(jax.ShapeDtypeStruct((rows, width), F32),) + (head,) * (num_tokens - 1),
        name="norm_backward",
    )(*sums, summed, gain, cotangent)


def finish_kernel(num_tokens, *refs):
    grad_ref, heads, out_ref = refs[0], refs[1:num_tokens], refs[num_tokens]
    me = lax.axis_index("tok")
    width = grad_ref.shape[1] // num_tokens
    own = head_slice(me, width)
    out_ref[0, :, own] = (2.0 * grad_ref[:, own]).astype(BF16)
    for s in range(1, num_tokens):
        place = head_slice(me ^ s, width)
        out_ref[0, :, place] = (grad_ref[:, place] + heads[s - 1][...].astype(F32)).astype(BF16)


def finish(grad_summed, heads):
    rows, width = grad_summed.shape
    num_tokens = lax.axis_size("tok")
    return pl.pallas_call(
        functools.partial(finish_kernel, num_tokens),
        out_shape=jax.ShapeDtypeStruct((1, rows, width), BF16),
        name="finish",
    )(grad_summed, *heads)


def shards(inputs, cotangent, norm_gain, router_weight, route_ids, w_gate, w_up, w_down):
    _, own, width = inputs.shape
    num_tokens = lax.axis_size("tok")
    size = lax.axis_size("dp")
    head = width // num_tokens
    experts = w_gate.shape[1]
    me = lax.axis_index("tok")

    heads = [
        exchange(lax.dynamic_slice(inputs[0], (0, (me ^ s) * head), (own, head)), "tok", s)
        for s in range(1, num_tokens)
    ]
    cot_chunks = gather_chunks(cotangent[0])
    normed, summed = norm_rows(inputs, norm_gain, heads)
    normed_chunks = gather_chunks(normed)
    back = back_hidden(cot_chunks, w_down)
    router_rows = router_weight[0].T
    pre_gate, pre_up, act, kept, sent, small = experts_backward(
        normed_chunks, w_gate, w_up, back, route_ids, router_rows, norm_gain
    )
    arrived = exchange(sent, "dp", 1)
    pair = (kept.astype(F32) + arrived.astype(F32)).astype(BF16)
    sums = [pair[0]] + [exchange(pair[s], "dp", 2 * s) for s in range(1, size // 2)]
    distance = 1
    while distance < size:
        small = small + exchange(small, "dp", distance)
        distance *= 2
    grad_gate, grad_up, grad_down = weight_gradients(normed_chunks, cot_chunks, pre_gate, pre_up, act)
    grad_summed, *sends = norm_backward(sums, summed, norm_gain, cotangent)
    returned = [exchange(sends[s - 1], "tok", s) for s in range(1, num_tokens)]
    grad_inputs = finish(grad_summed, returned)
    return (
        grad_inputs,
        grad_gate,
        grad_up,
        grad_down,
        small[:experts].T[None],
        small[experts][None],
    )


def solution(mesh):
    return jax.shard_map(
        shards,
        mesh=mesh,
        in_specs=(
            P("tok", "dp", None),
            P("tok", "dp", None),
            P("tok", None),
            P("tok", None, None),
            P("tok", None, None),
            P("tok", None, None, "dp"),
            P("tok", None, None, "dp"),
            P("tok", None, "dp", None),
        ),
        out_specs=(
            P("tok", "dp", None),
            P("tok", None, None, "dp"),
            P("tok", None, None, "dp"),
            P("tok", None, "dp", None),
            P("tok", None, None),
            P("tok", None),
        ),
        check_vma=False,
    )
```

```python
import functools

import jax
import jax.numpy as jnp
from jax import lax
from jax.experimental import pallas as pl
from jax.experimental.pallas import tpu as pltpu
from jax.sharding import PartitionSpec as P

BF16 = jnp.bfloat16
F32 = jnp.float32
MIB = 1024 * 1024


def dot(left, right, dims):
    return lax.dot_general(left, right, (dims, ((), ())), preferred_element_type=F32)


NN = ((1,), (0,))
NT = ((1,), (1,))
TN = ((0,), (0,))


def exchange(value, axis, distance):
    size = lax.axis_size(axis)
    return lax.ppermute(value, axis, [(i, i ^ distance) for i in range(size)])


def gather_chips(rows):
    size = lax.axis_size("dp")
    return [rows] + [exchange(rows, "dp", s) for s in range(2, size, 2)]


def gather_cores(chunks):
    return list(chunks) + [exchange(chunk, "dp", 1) for chunk in chunks]


def after(values):
    return lax.optimization_barrier(values)


def device_of(block, size):
    return 2 * block if block < size // 2 else 2 * block + 1 - size


def assemble(rows, chunks):
    for i, chunk in enumerate(chunks):
        own = chunk.shape[0]
        rows[i * own : (i + 1) * own] = chunk[...]


def head_slice(slot, width):
    return pl.ds(pl.multiple_of(slot * width, width), width)


def hbm(array):
    return pltpu.with_memory_space_constraint(array, pltpu.HBM)


def vmem(array):
    return pltpu.with_memory_space_constraint(array, pltpu.VMEM)


IN_HBM = pl.BlockSpec(memory_space=pltpu.HBM)
IN_VMEM = pl.BlockSpec(memory_space=pltpu.VMEM)
ANYWHERE = pl.BlockSpec(memory_space=pl.ANY)


def heads_kernel(x_hbm, cot_hbm, x_ref, cot_ref, *refs):
    sends, sems = refs[:-1], refs[-1]
    copy_x = pltpu.make_async_copy(x_hbm.at[0], x_ref, sems.at[0])
    copy_cot = pltpu.make_async_copy(cot_hbm.at[0], cot_ref, sems.at[1])
    copy_x.start()
    copy_cot.start()
    copy_x.wait()
    me = lax.axis_index("tok")
    width = sends[0].shape[1]
    for s, send in enumerate(sends):
        send[...] = x_ref[:, head_slice(me ^ (s + 1), width)]
    copy_cot.wait()


def split_heads(x, cotangent):
    _, rows, width = x.shape
    num_tokens = lax.axis_size("tok")
    head = jax.ShapeDtypeStruct((rows, width // num_tokens), BF16)
    return pl.pallas_call(
        heads_kernel,
        in_specs=[IN_HBM] * 2,
        out_shape=(jax.ShapeDtypeStruct((rows, width), BF16),) * 2 + (head,) * (num_tokens - 1),
        scratch_shapes=[pltpu.SemaphoreType.DMA((2,))],
        compiler_params=pltpu.CompilerParams(vmem_limit_bytes=4 * MIB),
        name="split_heads",
    )(hbm(x), hbm(cotangent))


def small_kernel(gain_hbm, router_hbm, route_hbm, gain_ref, router_ref, chosen_ref, routes, sems):
    copies = [
        pltpu.make_async_copy(src, dst, sems.at[i])
        for i, (src, dst) in enumerate(
            [
                (gain_hbm, gain_ref),
                (router_hbm, router_ref),
                (route_hbm, routes),
            ]
        )
    ]
    for copy in copies:
        copy.start()
    for copy in copies:
        copy.wait()
    rows, experts = chosen_ref.shape
    ids = lax.broadcasted_iota(jnp.int32, (experts, rows), 0)
    hit = routes[0:1, :] == ids
    for k in range(1, routes.shape[0]):
        hit = hit | (routes[k : k + 1, :] == ids)
    chosen_ref[...] = hit.astype(F32).T


def small_operands(gain, router_rows, routes):
    experts, all_rows = 8, routes.shape[1]
    return pl.pallas_call(
        small_kernel,
        in_specs=[IN_HBM] * 3,
        out_shape=(
            jax.ShapeDtypeStruct(gain.shape, F32),
            jax.ShapeDtypeStruct(router_rows.shape, BF16),
            jax.ShapeDtypeStruct((all_rows, experts), F32),
        ),
        scratch_shapes=[pltpu.VMEM(routes.shape, jnp.int32), pltpu.SemaphoreType.DMA((3,))],
        compiler_params=pltpu.CompilerParams(vmem_limit_bytes=4 * MIB),
        cost_estimate=pl.CostEstimate(flops=2**36, bytes_accessed=32 * MIB, transcendentals=0),
        name="small_operands",
    )(hbm(gain), hbm(router_rows), hbm(routes))


def norm_kernel(x_ref, gain_ref, *refs):
    heads, (normed_ref, summed_ref) = refs[:-2], refs[-2:]
    me = lax.axis_index("tok")
    width = heads[0].shape[1]
    own = head_slice(me, width)
    summed_ref[:, own] = 2.0 * x_ref[:, own].astype(F32)
    for s, head in enumerate(heads):
        place = head_slice(me ^ (s + 1), width)
        summed_ref[:, place] = x_ref[:, place].astype(F32) + head[...].astype(F32)
    summed = summed_ref[...]
    inv_rms = lax.rsqrt(jnp.mean(summed * summed, axis=1, keepdims=True) + 1e-06)
    normed_ref[...] = (summed * inv_rms * gain_ref[...]).astype(BF16)


def norm_rows(x, gain, heads):
    return pl.pallas_call(
        norm_kernel,
        out_shape=(jax.ShapeDtypeStruct(x.shape, BF16), jax.ShapeDtypeStruct(x.shape, F32)),
        compiler_params=pltpu.CompilerParams(vmem_limit_bytes=4 * MIB),
        name="norm_rows",
    )(x, gain, *heads)


def load_weights(refs, place, experts, sems):
    copies = []
    for i, (e, ref) in enumerate((e, ref) for e in experts for ref in refs):
        hidden = ref.shape[3]
        columns = pl.ds(i * hidden, hidden)
        copies.append(pltpu.make_async_copy(ref.at[0, e], place.at[:, columns], sems.at[i]))
        copies[-1].start()
    return copies


def back_kernel(size, *refs):
    chunks, (down_hbm, gate_hbm, up_hbm, back_ref, weights_ref) = refs[:size], refs[size : size + 5]
    cot, down, down_sems, sems = refs[size + 5 :]
    experts = down.shape[0]
    copies = [
        pltpu.make_async_copy(down_hbm.at[0, e], down.at[e], down_sems.at[e]) for e in range(experts)
    ]
    for copy in copies:
        copy.start()
    loads = load_weights((gate_hbm, up_hbm), weights_ref, range(experts // 2), sems)
    assemble(cot, chunks)
    for e in range(experts):
        copies[e].wait()
        back_ref[e] = dot(cot[...], down[e], NT)
    for load in loads:
        load.wait()


def back_hidden(chunks, w_down, w_gate, w_up):
    size = len(chunks)
    own, width = chunks[0].shape
    _, experts, hidden, _ = w_down.shape
    rows = size * own
    return pl.pallas_call(
        functools.partial(back_kernel, size),
        in_specs=[IN_VMEM] * size + [IN_HBM] * 3,
        out_specs=(IN_VMEM, ANYWHERE),
        out_shape=(
            jax.ShapeDtypeStruct((experts, rows, hidden), F32),
            jax.ShapeDtypeStruct((width, experts // 2 * 2 * hidden), BF16),
        ),
        scratch_shapes=[
            pltpu.VMEM((rows, width), BF16),
            pltpu.VMEM((experts, hidden, width), BF16),
            pltpu.SemaphoreType.DMA((experts,)),
            pltpu.SemaphoreType.DMA((experts // 2 * 2,)),
        ],
        compiler_params=pltpu.CompilerParams(vmem_limit_bytes=16 * MIB),
        cost_estimate=pl.CostEstimate(
            flops=2 * experts * rows * hidden * width,
            bytes_accessed=experts * hidden * (width * 4 + rows * 4) + rows * width * 2,
            transcendentals=0,
        ),
        name="back_hidden",
    )(*chunks, hbm(w_down), hbm(w_gate), hbm(w_up))


def expert_kernel(size, *refs):
    chunks, (first, gate_hbm, up_hbm, back_ref) = refs[:size], refs[size : size + 4]
    chosen_ref, router_ref, gain_ref, grads_out, act_out, sent_out = refs[size + 4 : size + 10]
    kept, (small_out, normed, second, sems) = refs[size + 10 : -4], refs[-4:]
    own, width = chunks[0].shape
    experts = router_ref.shape[0]
    hidden = back_ref.shape[2]
    split = experts // 2
    loads = load_weights((gate_hbm, up_hbm), second, range(split, experts), sems)
    assemble(normed, chunks)
    me = lax.axis_index("dp")
    hits = []
    for i in range(size):
        start = pl.multiple_of((me ^ device_of(i, size)) * own, own)
        hits.append(chosen_ref[pl.ds(start, own), :experts])
    chosen = jnp.concatenate(hits, axis=0)
    prob = jax.nn.sigmoid(dot(normed[...], router_ref[...], NT))
    gates = prob * chosen

    def forward(e):
        if e < split:
            return dot(normed[...], first[:, 2 * e * hidden : 2 * (e + 1) * hidden], NN)
        e -= split
        loads[2 * e].wait()
        loads[2 * e + 1].wait()
        return dot(normed[...], second[:, 2 * e * hidden : 2 * (e + 1) * hidden], NN)

    shares = []
    later = forward(0)
    for e in range(experts):
        pre_gate, pre_up = later[:, :hidden], later[:, hidden:]
        if e + 1 < experts:
            later = forward(e + 1)
        gate = gates[:, e : e + 1]
        back = back_ref[e]
        sigma = jax.nn.sigmoid(pre_gate)
        silu = pre_gate * sigma
        act = silu * pre_up
        shares.append(jnp.sum(act * back, axis=1, keepdims=True))
        scaled = gate * back
        grad_gate = scaled * pre_up * (sigma * (1.0 + pre_gate * (1.0 - sigma)))
        grads_out[:, 2 * e * hidden : (2 * e + 1) * hidden] = grad_gate.astype(BF16)
        grads_out[:, (2 * e + 1) * hidden : (2 * e + 2) * hidden] = (scaled * silu).astype(BF16)
        act_out[:, e * hidden : (e + 1) * hidden] = (gate * act).astype(BF16)
    coef = jnp.concatenate(shares, axis=1) * gates * (1.0 - prob)
    high = coef.astype(BF16).astype(F32)
    middle = (coef - high).astype(BF16).astype(F32)
    low = coef - high - middle
    terms = jnp.concatenate([high, middle, low], axis=1).astype(BF16)
    router = router_ref[...].astype(F32)
    router = jnp.concatenate([router] * 3, axis=0).astype(BF16)
    small = dot(terms, normed[...], TN)
    small_out[:experts] = small[:experts] + small[experts : 2 * experts] + small[2 * experts :]
    step = width // 4
    for c in range(0, width, step):
        here = slice(c, c + step)
        grad = dot(grads_out[:, : 2 * split * hidden], first[here, :], NT)
        grad = grad + dot(grads_out[:, 2 * split * hidden :], second[here, :], NT)
        grad = grad + dot(terms, router[:, here], NN)
        rows_here = normed[:, here].astype(F32)
        gain = jnp.sum(grad * rows_here, axis=0, keepdims=True) / gain_ref[:, here]
        small_out[experts:, here] = jnp.broadcast_to(gain, (8 - experts, step))
        grad = grad.astype(BF16)
        for i in range(size // 2):
            kept[i][:, here] = grad[i * own : (i + 1) * own]
        sent_out[:, here] = grad[size // 2 * own :]


def experts_backward(chunks, first, w_gate, w_up, back, chosen, router_rows, gain):
    size = len(chunks)
    own, width = chunks[0].shape
    experts, rows, hidden = back.shape
    kept = jax.ShapeDtypeStruct((own, width), BF16)
    return pl.pallas_call(
        functools.partial(expert_kernel, size),
        in_specs=[IN_VMEM] * (size + 1) + [IN_HBM] * 2 + [IN_VMEM] * 4,
        out_shape=(
            jax.ShapeDtypeStruct((rows, 2 * experts * hidden), BF16),
            jax.ShapeDtypeStruct((rows, experts * hidden), BF16),
            jax.ShapeDtypeStruct((rows // 2, width), BF16),
        )
        + (kept,) * (size // 2)
        + (jax.ShapeDtypeStruct((8, width), F32),),
        scratch_shapes=[
            pltpu.VMEM((rows, width), BF16),
            pltpu.VMEM((width, 2 * (experts - experts // 2) * hidden), BF16),
            pltpu.SemaphoreType.DMA((2 * (experts - experts // 2),)),
        ],
        compiler_params=pltpu.CompilerParams(vmem_limit_bytes=20 * MIB),
        cost_estimate=pl.CostEstimate(
            flops=8 * experts * rows * hidden * width,
            bytes_accessed=experts * hidden * (width * 4 + rows * 10) + rows * width * 4,
            transcendentals=experts * rows * hidden,
        ),
        name="experts_backward",
    )(*chunks, vmem(first), hbm(w_gate), hbm(w_up), back, chosen, router_rows, gain)


def pair_kernel(count, *refs):
    kept, (arrived_ref, small_ref, other_ref), outs = refs[:count], refs[count : count + 3], refs[count + 3 :]
    own = kept[0].shape[0]
    for i in range(count):
        arrived = arrived_ref[i * own : (i + 1) * own].astype(F32)
        outs[i][...] = (kept[i][...].astype(F32) + arrived).astype(BF16)
    outs[count][...] = small_ref[...] + other_ref[...]


def pair_sum(kept, arrived, small, other):
    return pl.pallas_call(
        functools.partial(pair_kernel, len(kept)),
        out_shape=tuple(jax.ShapeDtypeStruct(k.shape, BF16) for k in kept)
        + (jax.ShapeDtypeStruct(small.shape, F32),),
        compiler_params=pltpu.CompilerParams(vmem_limit_bytes=4 * MIB),
        name="pair_sum",
    )(*kept, arrived, small, other)


SLOTS = 4


def write_out(tiles, buffer, sems):
    copies = []
    for i, (value, destination) in enumerate(tiles):
        slot = i % SLOTS
        if i >= SLOTS:
            copies[i - SLOTS].wait()
        buffer[slot] = value().astype(BF16)
        copies.append(pltpu.make_async_copy(buffer.at[slot], destination, sems.at[slot]))
        copies[-1].start()
    for copy in copies[-SLOTS:]:
        copy.wait()


def gate_up_kernel(*refs):
    chunks, (grads_ref, gate_out, up_out, normed, buffer, sems) = refs[:-6], refs[-6:]
    assemble(normed, chunks)
    width = normed.shape[1]
    hidden = gate_out.shape[3]
    step = buffer.shape[1]
    tiles = []
    for e in range(gate_out.shape[1]):
        for i, out in enumerate((gate_out, up_out)):
            columns = slice((2 * e + i) * hidden, (2 * e + i + 1) * hidden)
            for c in range(0, width, step):
                value = lambda c=c, columns=columns: dot(normed[:, c : c + step], grads_ref[:, columns], TN)
                tiles.append((value, out.at[0, e, pl.ds(c, step)]))
    write_out(tiles, buffer, sems)


def down_kernel(*refs):
    chunks, (act_ref, down_out, cot, buffer, sems) = refs[:-5], refs[-5:]
    assemble(cot, chunks)
    hidden = down_out.shape[2]
    step = buffer.shape[1]
    tiles = []
    for e in range(down_out.shape[1]):
        for c in range(0, hidden, step):
            first = e * hidden + c
            value = lambda first=first: dot(act_ref[:, first : first + step], cot[...], TN)
            tiles.append((value, down_out.at[0, e, pl.ds(c, step)]))
    write_out(tiles, buffer, sems)


def weight_gradients(kernel, chunks, hidden_rows, shapes, step, name):
    width = chunks[0].shape[1]
    rows, columns = hidden_rows.shape
    out_bytes = sum(2 * shape[1] * shape[2] * shape[3] for shape in shapes)
    return pl.pallas_call(
        kernel,
        out_specs=(pl.BlockSpec(memory_space=pltpu.HBM),) * len(shapes),
        out_shape=tuple(jax.ShapeDtypeStruct(shape, BF16) for shape in shapes),
        scratch_shapes=[
            pltpu.VMEM((rows, width), BF16),
            pltpu.VMEM((SLOTS, step, shapes[0][3]), BF16),
            pltpu.SemaphoreType.DMA((SLOTS,)),
        ],
        compiler_params=pltpu.CompilerParams(vmem_limit_bytes=16 * MIB),
        cost_estimate=pl.CostEstimate(
            flops=2 * rows * columns * width,
            bytes_accessed=out_bytes + 2 * rows * (columns + width),
            transcendentals=0,
        ),
        name=name,
    )(*chunks, hidden_rows)


def norm_back_kernel(count, *refs):
    parts, (summed_ref, gain_ref, cot_ref, small_ref, other_ref) = refs[:count], refs[count : count + 5]
    grad_ref, total_ref = refs[count + 5 : count + 7]
    sends = refs[count + 7 :]
    grad_normed = parts[0][...].astype(F32)
    for part in parts[1:]:
        grad_normed = grad_normed + part[...].astype(F32)
    summed = summed_ref[...]
    inv_rms = lax.rsqrt(jnp.mean(summed * summed, axis=1, keepdims=True) + 1e-06)
    scaled = grad_normed * gain_ref[...]
    centre = jnp.mean(scaled * summed, axis=1, keepdims=True)
    grad = inv_rms * scaled - summed * (inv_rms * inv_rms * inv_rms * centre)
    grad_ref[...] = grad + cot_ref[...].astype(F32)
    me = lax.axis_index("tok")
    width = sends[0].shape[1]
    for s, send in enumerate(sends):
        send[...] = grad_ref[:, head_slice(me ^ (s + 1), width)].astype(BF16)
    total_ref[...] = small_ref[...] + other_ref[...]


def norm_backward(parts, summed, gain, cot, small, other):
    rows, width = summed.shape
    num_tokens = lax.axis_size("tok")
    head = jax.ShapeDtypeStruct((rows, width // num_tokens), BF16)
    return pl.pallas_call(
        functools.partial(norm_back_kernel, len(parts)),
        out_shape=(
            jax.ShapeDtypeStruct((rows, width), F32),
            jax.ShapeDtypeStruct(small.shape, F32),
        )
        + (head,) * (num_tokens - 1),
        compiler_params=pltpu.CompilerParams(vmem_limit_bytes=4 * MIB),
        name="norm_backward",
    )(*parts, summed, gain, cot, small, other)


def finish_kernel(grad_ref, small_ref, other_ref, *refs):
    heads, (out_ref, router_out, gain_out) = refs[:-3], refs[-3:]
    me = lax.axis_index("tok")
    width = heads[0].shape[1]
    experts = router_out.shape[0]
    own = head_slice(me, width)
    out_ref[0, :, own] = (2.0 * grad_ref[:, own]).astype(BF16)
    for s, head in enumerate(heads):
        place = head_slice(me ^ (s + 1), width)
        out_ref[0, :, place] = (grad_ref[:, place] + head[...].astype(F32)).astype(BF16)
    router_out[...] = small_ref[:experts] + other_ref[:experts]
    gain_out[...] = small_ref[experts : experts + 1] + other_ref[experts : experts + 1]


def finish(grad_summed, heads, small, other, experts):
    rows, width = grad_summed.shape
    return pl.pallas_call(
        finish_kernel,
        out_shape=(
            jax.ShapeDtypeStruct((1, rows, width), BF16),
            jax.ShapeDtypeStruct((experts, width), F32),
            jax.ShapeDtypeStruct((1, width), F32),
        ),
        compiler_params=pltpu.CompilerParams(vmem_limit_bytes=4 * MIB),
        name="finish",
    )(grad_summed, small, other, *heads)


def shards(inputs, cotangent, norm_gain, router_weight, route_ids, w_gate, w_up, w_down):
    width = inputs.shape[2]
    size = lax.axis_size("dp")
    experts = w_gate.shape[1]

    x, cot, *sends = split_heads(inputs, cotangent)
    heads = [exchange(v, "tok", s + 1) for s, v in enumerate(sends)]
    x, norm_gain = after((x, norm_gain))
    gain, router_rows, chosen = small_operands(norm_gain, router_weight[0].T, route_ids[0].T)
    heads, gain, router_rows, chosen = after((heads, gain, router_rows, chosen))
    far_cots = gather_chips(cot)
    normed, summed = norm_rows(x, gain, heads)
    far_rows = gather_chips(normed)
    cots = gather_cores(far_cots)
    back, weights = back_hidden(cots, w_down, w_gate, w_up)
    far_rows[1:], back = after((far_rows[1:], back))
    rows = gather_cores(far_rows)
    grads, act, sent, *kept, small = experts_backward(
        rows, weights, w_gate, w_up, back, chosen, router_rows, gain
    )
    arrived = exchange(sent, "dp", 1)
    *pairs, small = pair_sum(kept, arrived, small, exchange(small, "dp", 1))
    pairs, grads, small = after((pairs, grads, small))
    parts = pairs[:1] + [exchange(pair, "dp", 2 * s) for s, pair in enumerate(pairs) if s]
    distance = 2
    while 4 * distance < size:
        small = small + exchange(small, "dp", distance)
        distance *= 2
    other = exchange(small, "dp", distance)
    grad_gate, grad_up = weight_gradients(
        gate_up_kernel, rows, grads, (w_gate.shape, w_up.shape), width, "grad_gate_up"
    )
    parts, grad_gate, grad_up, other = after((parts, grad_gate, grad_up, other))
    grad_summed, small, *sends = norm_backward(parts, summed, gain, cot, small, other)
    sends, act, small = after((sends, act, small))
    returned = [exchange(v, "tok", s + 1) for s, v in enumerate(sends)]
    other = exchange(small, "dp", 2 * distance)
    (grad_down,) = weight_gradients(
        down_kernel, cots, act, (w_down.shape,), w_down.shape[2], "grad_down"
    )
    returned, grad_down, other = after((returned, grad_down, other))
    grad_inputs, grad_router, grad_gain = finish(grad_summed, returned, small, other, experts)
    return (
        grad_inputs,
        grad_gate,
        grad_up,
        grad_down,
        grad_router.T[None],
        grad_gain,
    )


def solution(mesh):
    return jax.shard_map(
        shards,
        mesh=mesh,
        in_specs=(
            P("tok", "dp", None),
            P("tok", "dp", None),
            P("tok", None),
            P("tok", None, None),
            P("tok", None, None),
            P("tok", None, None, "dp"),
            P("tok", None, None, "dp"),
            P("tok", None, "dp", None),
        ),
        out_specs=(
            P("tok", "dp", None),
            P("tok", None, None, "dp"),
            P("tok", None, None, "dp"),
            P("tok", None, "dp", None),
            P("tok", None, None),
            P("tok", None),
        ),
        check_vma=False,
    )
```

```python
import functools

import jax
import jax.numpy as jnp
from jax import lax
from jax.experimental import pallas as pl
from jax.experimental.pallas import tpu as pltpu
from jax.sharding import PartitionSpec as P

BF16 = jnp.bfloat16
F32 = jnp.float32
MIB = 1024 * 1024


def dot(left, right, dims):
    return lax.dot_general(left, right, (dims, ((), ())), preferred_element_type=F32)


NN = ((1,), (0,))
NT = ((1,), (1,))
TN = ((0,), (0,))


def exchange(value, axis, distance):
    size = lax.axis_size(axis)
    return lax.ppermute(value, axis, [(i, i ^ distance) for i in range(size)])


def gather_chips(rows):
    size = lax.axis_size("dp")
    return [rows] + [exchange(rows, "dp", s) for s in range(2, size, 2)]


def gather_cores(chunks):
    return list(chunks) + [exchange(chunk, "dp", 1) for chunk in chunks]


def after(values):
    return lax.optimization_barrier(values)


def device_of(block, size):
    return 2 * block if block < size // 2 else 2 * block + 1 - size


def assemble(rows, chunks):
    first = 0
    for chunk in chunks:
        rows[first : first + chunk.shape[0]] = chunk[...]
        first += chunk.shape[0]


def head_slice(slot, width):
    return pl.ds(pl.multiple_of(slot * width, width), width)


def hbm(array):
    return pltpu.with_memory_space_constraint(array, pltpu.HBM)


def vmem(array):
    return pltpu.with_memory_space_constraint(array, pltpu.VMEM)


IN_HBM = pl.BlockSpec(memory_space=pltpu.HBM)
IN_VMEM = pl.BlockSpec(memory_space=pltpu.VMEM)
ANYWHERE = pl.BlockSpec(memory_space=pl.ANY)


def head_plan(num_tokens):
    held, stages, bit = [(0, d) for d in range(1, num_tokens)], [], 1
    while bit < num_tokens:
        sent = [item for item in held if item[1] & bit]
        received = [(source ^ bit, target ^ bit) for source, target in sent]
        held = [item for item in held if not item[1] & bit] + received
        stages.append((bit, sent, received))
        bit *= 2
    first = stages[0][1]
    return first, [(0, d) for d in range(1, num_tokens) if (0, d) not in first], stages


def pick(item, lists):
    for i, items in enumerate(lists):
        if item in items:
            return i, items.index(item)


def pack_kernel(picks, *refs):
    for k, (i, j) in enumerate(picks):
        refs[-1][k] = refs[i][j]


def pack_heads(arrays, picks):
    return pl.pallas_call(
        functools.partial(pack_kernel, picks),
        out_shape=jax.ShapeDtypeStruct((len(picks),) + arrays[0].shape[1:], BF16),
        compiler_params=pltpu.CompilerParams(vmem_limit_bytes=4 * MIB),
        name="pack_heads",
    )(*arrays)


def first_stage(first, kept):
    _, kept_items, stages = head_plan(lax.axis_size("tok"))
    bit, _, received = stages[0]
    return [kept, exchange(first, "tok", bit)], [kept_items, received]


def other_stages(arrays, lists):
    for bit, sent, received in head_plan(lax.axis_size("tok"))[2][1:]:
        payload = pack_heads(arrays, [pick(item, lists) for item in sent])
        arrays = arrays + [exchange(payload, "tok", bit)]
        lists = lists + [received]
    return arrays, lists


def heads_kernel(x_hbm, cot_hbm, x_ref, cot_ref, first_ref, kept_ref, sems):
    copy_x = pltpu.make_async_copy(x_hbm.at[0], x_ref, sems.at[0])
    copy_cot = pltpu.make_async_copy(cot_hbm.at[0], cot_ref, sems.at[1])
    copy_x.start()
    copy_cot.start()
    copy_x.wait()
    store_heads(x_ref, first_ref, kept_ref)
    copy_cot.wait()


def store_heads(rows_ref, first_ref, kept_ref):
    width = first_ref.shape[2]
    first, kept, _ = head_plan(rows_ref.shape[1] // width)
    me = lax.axis_index("tok")
    for ref, items in ((first_ref, first), (kept_ref, kept)):
        for k, (_, d) in enumerate(items):
            ref[k] = rows_ref[:, head_slice(me ^ d, width)].astype(BF16)


def head_shapes(rows, width):
    num_tokens = lax.axis_size("tok")
    first, kept, _ = head_plan(num_tokens)
    return tuple(
        jax.ShapeDtypeStruct((len(items), rows, width // num_tokens), BF16) for items in (first, kept)
    )


def split_heads(x, cotangent):
    _, rows, width = x.shape
    return pl.pallas_call(
        heads_kernel,
        in_specs=[IN_HBM] * 2,
        out_shape=(jax.ShapeDtypeStruct((rows, width), BF16),) * 2 + head_shapes(rows, width),
        scratch_shapes=[pltpu.SemaphoreType.DMA((2,))],
        compiler_params=pltpu.CompilerParams(vmem_limit_bytes=4 * MIB),
        name="split_heads",
    )(hbm(x), hbm(cotangent))


def from_tokens(arrays, lists):
    num_tokens = lax.axis_size("tok")
    return tuple((d,) + pick((d, 0), lists) for d in range(1, num_tokens))


def small_kernel(gain_hbm, router_hbm, route_hbm, down_hbm, *refs):
    gain_ref, router_ref, chosen_ref, down_ref, routes, sems, down_sem = refs
    load = pltpu.make_async_copy(down_hbm.at[0, pl.ds(0, down_ref.shape[0])], down_ref, down_sem)
    load.start()
    copies = [
        pltpu.make_async_copy(src, dst, sems.at[i])
        for i, (src, dst) in enumerate(
            [
                (gain_hbm, gain_ref),
                (router_hbm, router_ref),
                (route_hbm, routes),
            ]
        )
    ]
    for copy in copies:
        copy.start()
    for copy in copies:
        copy.wait()
    rows, experts = chosen_ref.shape
    ids = lax.broadcasted_iota(jnp.int32, (experts, rows), 0)
    hit = routes[0:1, :] == ids
    for k in range(1, routes.shape[0]):
        hit = hit | (routes[k : k + 1, :] == ids)
    chosen_ref[...] = hit.astype(F32).T
    load.wait()


def small_operands(gain, router_rows, routes, w_down):
    experts, all_rows = 8, routes.shape[1]
    return pl.pallas_call(
        small_kernel,
        in_specs=[IN_HBM] * 4,
        out_specs=(IN_VMEM,) * 3 + (ANYWHERE,),
        out_shape=(
            jax.ShapeDtypeStruct(gain.shape, F32),
            jax.ShapeDtypeStruct(router_rows.shape, BF16),
            jax.ShapeDtypeStruct((all_rows, experts), F32),
            jax.ShapeDtypeStruct((w_down.shape[1] // 2,) + w_down.shape[2:], BF16),
        ),
        scratch_shapes=[
            pltpu.VMEM(routes.shape, jnp.int32),
            pltpu.SemaphoreType.DMA((3,)),
            pltpu.SemaphoreType.DMA(()),
        ],
        compiler_params=pltpu.CompilerParams(vmem_limit_bytes=4 * MIB),
        cost_estimate=pl.CostEstimate(flops=2**36, bytes_accessed=32 * MIB, transcendentals=0),
        name="small_operands",
    )(hbm(gain), hbm(router_rows), hbm(routes), hbm(w_down))


def norm_kernel(places, x_ref, gain_ref, *refs):
    heads, (normed_ref, summed_ref) = refs[:-2], refs[-2:]
    me = lax.axis_index("tok")
    width = heads[0].shape[2]
    own = head_slice(me, width)
    summed_ref[:, own] = 2.0 * x_ref[:, own].astype(F32)
    for d, i, j in places:
        place = head_slice(me ^ d, width)
        summed_ref[:, place] = x_ref[:, place].astype(F32) + heads[i][j].astype(F32)
    summed = summed_ref[...]
    inv_rms = lax.rsqrt(jnp.mean(summed * summed, axis=1, keepdims=True) + 1e-06)
    normed_ref[...] = (summed * inv_rms * gain_ref[...]).astype(BF16)


def norm_rows(x, gain, heads, places):
    return pl.pallas_call(
        functools.partial(norm_kernel, places),
        out_shape=(jax.ShapeDtypeStruct(x.shape, BF16), jax.ShapeDtypeStruct(x.shape, F32)),
        compiler_params=pltpu.CompilerParams(vmem_limit_bytes=4 * MIB),
        name="norm_rows",
    )(x, gain, *heads)


def join_kernel(*refs):
    assemble(refs[-1], refs[:-1])


def join_rows(chunks):
    rows, width = sum(chunk.shape[0] for chunk in chunks), chunks[0].shape[1]
    return pl.pallas_call(
        join_kernel,
        out_shape=jax.ShapeDtypeStruct((rows, width), BF16),
        compiler_params=pltpu.CompilerParams(vmem_limit_bytes=4 * MIB),
        name="join_rows",
    )(*chunks)


def load_weights(refs, place, experts, sems):
    copies = []
    for i, (e, ref) in enumerate((e, ref) for e in experts for ref in refs):
        hidden = ref.shape[3]
        columns = pl.ds(i * hidden, hidden)
        copies.append(pltpu.make_async_copy(ref.at[0, e], place.at[:, columns], sems.at[i]))
        copies[-1].start()
    return copies


def back_kernel(count, *refs):
    chunks, (first, down_hbm, gate_hbm, up_hbm, back_ref, weights_ref) = refs[:count], refs[count : count + 6]
    cot, second, down_sems, sems = refs[count + 6 :]
    split = first.shape[0]
    experts = split + second.shape[0]
    copies = [
        pltpu.make_async_copy(down_hbm.at[0, split + e], second.at[e], down_sems.at[e])
        for e in range(experts - split)
    ]
    for copy in copies:
        copy.start()
    loads = load_weights((gate_hbm, up_hbm), weights_ref, range(experts // 2), sems)
    assemble(cot, chunks)
    for e in range(split):
        back_ref[e] = dot(cot[...], first[e], NT)
    for e, copy in enumerate(copies):
        copy.wait()
        back_ref[split + e] = dot(cot[...], second[e], NT)
    for load in loads:
        load.wait()


def back_hidden(chunks, first, w_down, w_gate, w_up):
    _, experts, hidden, width = w_down.shape
    rows = sum(chunk.shape[0] for chunk in chunks)
    rest = experts - first.shape[0]
    return pl.pallas_call(
        functools.partial(back_kernel, len(chunks)),
        in_specs=[IN_VMEM] * (len(chunks) + 1) + [IN_HBM] * 3,
        out_specs=(IN_VMEM, ANYWHERE),
        out_shape=(
            jax.ShapeDtypeStruct((experts, rows, hidden), F32),
            jax.ShapeDtypeStruct((width, experts // 2 * 2 * hidden), BF16),
        ),
        scratch_shapes=[
            pltpu.VMEM((rows, width), BF16),
            pltpu.VMEM((rest, hidden, width), BF16),
            pltpu.SemaphoreType.DMA((rest,)),
            pltpu.SemaphoreType.DMA((experts // 2 * 2,)),
        ],
        compiler_params=pltpu.CompilerParams(vmem_limit_bytes=16 * MIB),
        cost_estimate=pl.CostEstimate(
            flops=0,
            bytes_accessed=0,
            transcendentals=0,
        ),
        name="back_hidden",
    )(*chunks, vmem(first), hbm(w_down), hbm(w_gate), hbm(w_up))


def expert_kernel(size, *refs):
    chunks, (first, gate_hbm, up_hbm, back_ref) = refs[:size], refs[size : size + 4]
    chosen_ref, router_ref, gain_ref, grads_out, act_out, sent_out = refs[size + 4 : size + 10]
    kept, (small_out, normed, second, sems) = refs[size + 10 : -4], refs[-4:]
    own, width = chunks[0].shape
    experts = router_ref.shape[0]
    hidden = back_ref.shape[2]
    split = experts // 2
    loads = load_weights((gate_hbm, up_hbm), second, range(split, experts), sems)
    assemble(normed, chunks)
    me = lax.axis_index("dp")
    hits = []
    for i in range(size):
        start = pl.multiple_of((me ^ device_of(i, size)) * own, own)
        hits.append(chosen_ref[pl.ds(start, own), :experts])
    chosen = jnp.concatenate(hits, axis=0)
    prob = jax.nn.sigmoid(dot(normed[...], router_ref[...], NT))
    gates = prob * chosen

    def forward(e):
        if e < split:
            return dot(normed[...], first[:, 2 * e * hidden : 2 * (e + 1) * hidden], NN)
        e -= split
        loads[2 * e].wait()
        loads[2 * e + 1].wait()
        return dot(normed[...], second[:, 2 * e * hidden : 2 * (e + 1) * hidden], NN)

    shares = []
    later = forward(0)
    for e in range(experts):
        pre_gate, pre_up = later[:, :hidden], later[:, hidden:]
        if e + 1 < experts:
            later = forward(e + 1)
        gate = gates[:, e : e + 1]
        back = back_ref[e]
        sigma = jax.nn.sigmoid(pre_gate)
        silu = pre_gate * sigma
        act = silu * pre_up
        shares.append(jnp.sum(act * back, axis=1, keepdims=True))
        scaled = gate * back
        grad_gate = scaled * pre_up * (sigma * (1.0 + pre_gate * (1.0 - sigma)))
        grads_out[:, 2 * e * hidden : (2 * e + 1) * hidden] = grad_gate.astype(BF16)
        grads_out[:, (2 * e + 1) * hidden : (2 * e + 2) * hidden] = (scaled * silu).astype(BF16)
        act_out[:, e * hidden : (e + 1) * hidden] = (gate * act).astype(BF16)
    coef = jnp.concatenate(shares, axis=1) * gates * (1.0 - prob)
    high = coef.astype(BF16).astype(F32)
    middle = (coef - high).astype(BF16).astype(F32)
    low = coef - high - middle
    terms = jnp.concatenate([high, middle, low], axis=1).astype(BF16)
    router = router_ref[...].astype(F32)
    router = jnp.concatenate([router] * 3, axis=0).astype(BF16)
    small = dot(terms, normed[...], TN)
    small_out[:experts] = small[:experts] + small[experts : 2 * experts] + small[2 * experts :]
    half = size // 2 * own
    step = width // 4
    for c in range(0, width, step):
        here = slice(c, c + step)
        grad = dot(grads_out[:, : 2 * split * hidden], first[here, :], NT)
        grad = grad + dot(grads_out[:, 2 * split * hidden :], second[here, :], NT)
        grad = grad + dot(terms, router[:, here], NN)
        rows_here = normed[:, here].astype(F32)
        gain = jnp.sum(grad * rows_here, axis=0, keepdims=True) / gain_ref[:, here]
        small_out[experts:, here] = jnp.broadcast_to(gain, (8 - experts, step))
        grad = grad.astype(BF16)
        for i in range(size // 2):
            kept[i][:, here] = grad[i * own : (i + 1) * own]
        sent_out[:half, here] = grad[half:]
    core = me % 2
    sent_out[half:] = two_terms(small_out[:, head_slice(1 - core, width // 2)])


def experts_backward(chunks, first, w_gate, w_up, back, chosen, router_rows, gain):
    size = len(chunks)
    own, width = chunks[0].shape
    experts, rows, hidden = back.shape
    kept = jax.ShapeDtypeStruct((own, width), BF16)
    return pl.pallas_call(
        functools.partial(expert_kernel, size),
        in_specs=[IN_VMEM] * (size + 1) + [IN_HBM] * 2 + [IN_VMEM] * 4,
        out_shape=(
            jax.ShapeDtypeStruct((rows, 2 * experts * hidden), BF16),
            jax.ShapeDtypeStruct((rows, experts * hidden), BF16),
            jax.ShapeDtypeStruct((rows // 2 + 8, width), BF16),
        )
        + (kept,) * (size // 2)
        + (jax.ShapeDtypeStruct((8, width), F32),),
        scratch_shapes=[
            pltpu.VMEM((rows, width), BF16),
            pltpu.VMEM((width, 2 * (experts - experts // 2) * hidden), BF16),
            pltpu.SemaphoreType.DMA((2 * (experts - experts // 2),)),
        ],
        compiler_params=pltpu.CompilerParams(vmem_limit_bytes=20 * MIB),
        cost_estimate=pl.CostEstimate(
            flops=8 * experts * rows * hidden * width,
            bytes_accessed=experts * hidden * (width * 4 + rows * 10) + rows * width * 4,
            transcendentals=experts * rows * hidden,
        ),
        name="experts_backward",
    )(*chunks, vmem(first), hbm(w_gate), hbm(w_up), back, chosen, router_rows, gain)


def two_terms(small):
    high = small.astype(BF16)
    low = (small - high.astype(F32)).astype(BF16)
    return jnp.concatenate([high, low], axis=1)


def one_term(terms):
    half = terms.shape[1] // 2
    return terms[:, :half].astype(F32) + terms[:, half:].astype(F32)


def pair_kernel(count, *refs):
    kept, (arrived_ref, small_ref), outs = refs[:count], refs[count : count + 2], refs[count + 2 :]
    own, width = kept[0].shape
    core = lax.axis_index("dp") % 2
    mine = small_ref[:, head_slice(core, width // 2)]
    small = two_terms(mine + one_term(arrived_ref[count * own :]))
    for i in range(count):
        arrived = arrived_ref[i * own : (i + 1) * own].astype(F32)
        outs[i][:own] = (kept[i][...].astype(F32) + arrived).astype(BF16)
        outs[i][own:] = small


def pair_sum(kept, arrived, small):
    own, width = kept[0].shape
    return pl.pallas_call(
        functools.partial(pair_kernel, len(kept)),
        out_shape=(jax.ShapeDtypeStruct((own + 8, width), BF16),) * len(kept),
        compiler_params=pltpu.CompilerParams(vmem_limit_bytes=4 * MIB),
        name="pair_sum",
    )(*kept, arrived, small)


SLOTS = 4


def write_out(tiles, buffer, sems):
    copies = []
    for i, (value, destination) in enumerate(tiles):
        slot = i % SLOTS
        if i >= SLOTS:
            copies[i - SLOTS].wait()
        buffer[slot] = value().astype(BF16)
        copies.append(pltpu.make_async_copy(buffer.at[slot], destination, sems.at[slot]))
        copies[-1].start()
    for copy in copies[-SLOTS:]:
        copy.wait()


def gate_up_kernel(*refs):
    chunks, (grads_ref, gate_out, up_out, normed, buffer, sems) = refs[:-6], refs[-6:]
    assemble(normed, chunks)
    width = normed.shape[1]
    hidden = gate_out.shape[3]
    step = buffer.shape[1]
    tiles = []
    for e in range(gate_out.shape[1]):
        for i, out in enumerate((gate_out, up_out)):
            columns = slice((2 * e + i) * hidden, (2 * e + i + 1) * hidden)
            for c in range(0, width, step):
                value = lambda c=c, columns=columns: dot(normed[:, c : c + step], grads_ref[:, columns], TN)
                tiles.append((value, out.at[0, e, pl.ds(c, step)]))
    write_out(tiles, buffer, sems)


def down_kernel(experts, *refs):
    cot, buffer, sems = refs[-3:]
    down_out, (*chunks, act_ref) = refs[-4], refs[: -5 if experts[0] else -4]
    assemble(cot, chunks)
    hidden = down_out.shape[2]
    tiles = []
    for e in experts:
        value = lambda e=e: dot(act_ref[:, e * hidden : (e + 1) * hidden], cot[...], TN)
        tiles.append((value, down_out.at[0, e]))
    write_out(tiles, buffer, sems)


def weight_gradients(kernel, chunks, hidden_rows, shapes, name, share=1.0, started=None):
    width = chunks[0].shape[1]
    rows, columns = hidden_rows.shape
    out_bytes = sum(2 * shape[1] * shape[2] * shape[3] for shape in shapes)
    operands = (*chunks, hidden_rows) + (() if started is None else (started,))
    return pl.pallas_call(
        kernel,
        in_specs=[IN_VMEM] * (len(chunks) + 1) + [IN_HBM] * (started is not None),
        out_specs=(IN_HBM,) * len(shapes),
        out_shape=tuple(jax.ShapeDtypeStruct(shape, BF16) for shape in shapes),
        input_output_aliases={} if started is None else {len(operands) - 1: 0},
        scratch_shapes=[
            pltpu.VMEM((rows, width), BF16),
            pltpu.VMEM((SLOTS,) + shapes[0][2:], BF16),
            pltpu.SemaphoreType.DMA((SLOTS,)),
        ],
        compiler_params=pltpu.CompilerParams(vmem_limit_bytes=16 * MIB),
        cost_estimate=pl.CostEstimate(
            flops=int(share * 2 * rows * columns * width),
            bytes_accessed=int(share * out_bytes) + 2 * rows * (columns + width),
            transcendentals=0,
        ),
        name=name,
    )(*operands)


def norm_back_kernel(count, *refs):
    parts, (summed_ref, gain_ref, cot_ref) = refs[:count], refs[count : count + 3]
    grad_ref, small_out, *sends = refs[count + 3 :]
    own = summed_ref.shape[0]
    grad_normed = parts[0][:own].astype(F32)
    for part in parts[1:]:
        grad_normed = grad_normed + part[:own].astype(F32)
    summed = summed_ref[...]
    inv_rms = lax.rsqrt(jnp.mean(summed * summed, axis=1, keepdims=True) + 1e-06)
    scaled = grad_normed * gain_ref[...]
    centre = jnp.mean(scaled * summed, axis=1, keepdims=True)
    grad = inv_rms * scaled - summed * (inv_rms * inv_rms * inv_rms * centre)
    grad_ref[...] = grad + cot_ref[...].astype(F32)
    head = sends[0].shape[2]
    for s, send in enumerate(sends):
        place = head_slice(lax.axis_index("tok") ^ (s + 1), head)
        send[0] = grad_ref[:, place].astype(BF16)
    me = lax.axis_index("dp") // 2
    smalls = jnp.stack([one_term(part[own:]) for part in parts])
    small = jnp.zeros(smalls.shape[1:], F32)
    for chip in range(count):
        for i in range(count):
            small = small + jnp.where((me ^ i) == chip, smalls[i], 0.0)
    small_out[...] = small


def norm_backward(parts, summed, gain, cot):
    rows, width = summed.shape
    num_tokens = lax.axis_size("tok")
    head = jax.ShapeDtypeStruct((1, rows, width // num_tokens), BF16)
    return pl.pallas_call(
        functools.partial(norm_back_kernel, len(parts)),
        out_shape=(
            jax.ShapeDtypeStruct((rows, width), F32),
            jax.ShapeDtypeStruct((8, width // 2), F32),
        )
        + (head,) * (num_tokens - 1),
        compiler_params=pltpu.CompilerParams(vmem_limit_bytes=4 * MIB),
        name="norm_backward",
    )(*parts, summed, gain, cot)


def finish_kernel(places, grad_ref, small_ref, other_ref, *refs):
    heads, (out_ref, router_out, gain_out) = refs[:-3], refs[-3:]
    core = lax.axis_index("dp") % 2
    experts, columns = router_out.shape
    for ref, c in ((small_ref, core), (other_ref, 1 - core)):
        place = head_slice(c, columns // 2)
        router_out[:, place] = ref[:experts]
        gain_out[:, place] = ref[experts : experts + 1]
    me = lax.axis_index("tok")
    width = heads[0].shape[2]
    own = head_slice(me, width)
    out_ref[0, :, own] = (2.0 * grad_ref[:, own]).astype(BF16)
    for d, i, j in places:
        place = head_slice(me ^ d, width)
        out_ref[0, :, place] = (grad_ref[:, place] + heads[i][j].astype(F32)).astype(BF16)


def finish(grad_summed, heads, places, small, other, experts):
    rows, width = grad_summed.shape
    return pl.pallas_call(
        functools.partial(finish_kernel, places),
        out_shape=(
            jax.ShapeDtypeStruct((1, rows, width), BF16),
            jax.ShapeDtypeStruct((experts, width), F32),
            jax.ShapeDtypeStruct((1, width), F32),
        ),
        compiler_params=pltpu.CompilerParams(vmem_limit_bytes=4 * MIB),
        name="finish",
    )(grad_summed, small, other, *heads)


def shards(inputs, cotangent, norm_gain, router_weight, route_ids, w_gate, w_up, w_down):
    width = inputs.shape[2]
    size = lax.axis_size("dp")
    experts = w_gate.shape[1]

    x, cot, first, kept = split_heads(inputs, cotangent)
    heads, items = first_stage(first, kept)
    heads, items = other_stages(heads, items)
    cots, distance = [cot], 2
    while distance < size:
        cots += [exchange(chunk, "dp", distance) for chunk in cots]
        distance *= 2
    norm_gain, heads[1] = after((norm_gain, heads[1]))
    gain, router_rows, chosen, down = small_operands(
        norm_gain, router_weight[0].T, route_ids[0].T, w_down
    )
    heads, gain, router_rows, chosen, down = after((heads, gain, router_rows, chosen, down))
    places = from_tokens(heads, items)
    normed, summed = norm_rows(x, gain, heads, places)
    far_rows = gather_chips(normed)
    cots, summed = after((cots, summed))
    cots = gather_cores([join_rows(cots)])
    back, weights = back_hidden(cots, down, w_down, w_gate, w_up)
    far_rows[1:], back = after((far_rows[1:], back))
    rows = gather_cores(far_rows)
    grads, act, sent, *kept, small = experts_backward(
        rows, weights, w_gate, w_up, back, chosen, router_rows, gain
    )
    sent, act = after((sent, act))
    arrived = exchange(sent, "dp", 1)
    (grad_down,) = weight_gradients(
        functools.partial(down_kernel, range(1)), cots, act, (w_down.shape,), "grad_down_0", 1 / experts
    )
    arrived, grad_down, grads = after((arrived, grad_down, grads))
    pairs = pair_sum(kept, arrived, small)
    pairs, grads = after((pairs, grads))
    parts = [pairs[0]] + [exchange(pair, "dp", 2 * s) for s, pair in enumerate(pairs) if s]
    grad_gate, grad_up = weight_gradients(
        gate_up_kernel, rows, grads, (w_gate.shape, w_up.shape), "grad_gate_up"
    )
    parts, grad_gate, grad_up = after((parts, grad_gate, grad_up))
    grad_summed, small, *sends = norm_backward(parts, summed, gain, cot)
    sends, act, small = after((sends, act, small))
    other = exchange(small, "dp", 1)
    returned = [exchange(send, "tok", s + 1) for s, send in enumerate(sends)]
    (grad_down,) = weight_gradients(
        functools.partial(down_kernel, range(1, experts)),
        cots,
        act,
        (w_down.shape,),
        "grad_down",
        1 - 1 / experts,
        grad_down,
    )
    returned, grad_down, other = after((returned, grad_down, other))
    places = tuple((s + 1, s, 0) for s in range(len(returned)))
    grad_inputs, grad_router, grad_gain = finish(grad_summed, returned, places, small, other, experts)
    return (
        grad_inputs,
        grad_gate,
        grad_up,
        grad_down,
        grad_router.T[None],
        grad_gain,
    )


def solution(mesh):
    return jax.shard_map(
        shards,
        mesh=mesh,
        in_specs=(
            P("tok", "dp", None),
            P("tok", "dp", None),
            P("tok", None),
            P("tok", None, None),
            P("tok", None, None),
            P("tok", None, None, "dp"),
            P("tok", None, None, "dp"),
            P("tok", None, "dp", None),
        ),
        out_specs=(
            P("tok", "dp", None),
            P("tok", None, None, "dp"),
            P("tok", None, None, "dp"),
            P("tok", None, "dp", None),
            P("tok", None, None),
            P("tok", None),
        ),
        check_vma=False,
    )
```

```python
import functools
import math

import jax
import jax.numpy as jnp
from jax import lax
from jax.experimental import pallas as pl
from jax.experimental.pallas import tpu as pltpu
from jax.sharding import PartitionSpec as P

BF16 = jnp.bfloat16
F32 = jnp.float32
MIB = 1024 * 1024


def dot(left, right, dims):
    return lax.dot_general(left, right, (dims, ((), ())), preferred_element_type=F32)


NN = ((1,), (0,))
NT = ((1,), (1,))
TN = ((0,), (0,))


def exchange(value, axis, distance):
    size = lax.axis_size(axis)
    return lax.ppermute(value, axis, [(i, i ^ distance) for i in range(size)])


def gather_chips(rows):
    size = lax.axis_size("dp")
    return [rows] + [exchange(rows, "dp", s) for s in range(2, size, 2)]


def gather_cores(chunks):
    return list(chunks) + [exchange(chunk, "dp", 1) for chunk in chunks]


def after(values):
    return lax.optimization_barrier(values)


def device_of(block, size):
    return 2 * block if block < size // 2 else 2 * block + 1 - size


def assemble(rows, chunks):
    first = 0
    for chunk in chunks:
        rows[first : first + chunk.shape[0]] = chunk[...]
        first += chunk.shape[0]


def head_slice(slot, width):
    return pl.ds(pl.multiple_of(slot * width, width), width)


def hbm(array):
    return pltpu.with_memory_space_constraint(array, pltpu.HBM)


def vmem(array):
    return pltpu.with_memory_space_constraint(array, pltpu.VMEM)


IN_HBM = pl.BlockSpec(memory_space=pltpu.HBM)
IN_VMEM = pl.BlockSpec(memory_space=pltpu.VMEM)
ANYWHERE = pl.BlockSpec(memory_space=pl.ANY)


def head_plan(num_tokens):
    held, stages, bit = [(0, d) for d in range(1, num_tokens)], [], 1
    while bit < num_tokens:
        sent = [item for item in held if item[1] & bit]
        received = [(source ^ bit, target ^ bit) for source, target in sent]
        held = [item for item in held if not item[1] & bit] + received
        stages.append((bit, sent, received))
        bit *= 2
    first = stages[0][1]
    return first, [(0, d) for d in range(1, num_tokens) if (0, d) not in first], stages


def pick(item, lists):
    for i, items in enumerate(lists):
        if item in items:
            return i, items.index(item)


def pack_kernel(picks, *refs):
    for k, (i, j) in enumerate(picks):
        refs[-1][k] = refs[i][j]


def pack_heads(arrays, picks):
    return pl.pallas_call(
        functools.partial(pack_kernel, picks),
        out_shape=jax.ShapeDtypeStruct((len(picks),) + arrays[0].shape[1:], BF16),
        compiler_params=pltpu.CompilerParams(vmem_limit_bytes=4 * MIB),
        name="pack_heads",
    )(*arrays)


def first_stage(first, kept):
    _, kept_items, stages = head_plan(lax.axis_size("tok"))
    bit, _, received = stages[0]
    return [kept, exchange(first, "tok", bit)], [kept_items, received]


def other_stages(arrays, lists):
    for bit, sent, received in head_plan(lax.axis_size("tok"))[2][1:]:
        payload = pack_heads(arrays, [pick(item, lists) for item in sent])
        arrays = arrays + [exchange(payload, "tok", bit)]
        lists = lists + [received]
    return arrays, lists


def heads_kernel(x_hbm, cot_hbm, x_ref, cot_ref, first_ref, kept_ref, sems):
    copy_x = pltpu.make_async_copy(x_hbm.at[0], x_ref, sems.at[0])
    copy_cot = pltpu.make_async_copy(cot_hbm.at[0], cot_ref, sems.at[1])
    copy_x.start()
    copy_cot.start()
    copy_x.wait()
    store_heads(x_ref, first_ref, kept_ref)
    copy_cot.wait()


def store_heads(rows_ref, first_ref, kept_ref):
    width = first_ref.shape[2]
    first, kept, _ = head_plan(rows_ref.shape[1] // width)
    me = lax.axis_index("tok")
    for ref, items in ((first_ref, first), (kept_ref, kept)):
        for k, (_, d) in enumerate(items):
            ref[k] = rows_ref[:, head_slice(me ^ d, width)].astype(BF16)


def head_shapes(rows, width):
    num_tokens = lax.axis_size("tok")
    first, kept, _ = head_plan(num_tokens)
    return tuple(
        jax.ShapeDtypeStruct((len(items), rows, width // num_tokens), BF16) for items in (first, kept)
    )


def split_heads(x, cotangent):
    _, rows, width = x.shape
    return pl.pallas_call(
        heads_kernel,
        in_specs=[IN_HBM] * 2,
        out_shape=(jax.ShapeDtypeStruct((rows, width), BF16),) * 2 + head_shapes(rows, width),
        scratch_shapes=[pltpu.SemaphoreType.DMA((2,))],
        compiler_params=pltpu.CompilerParams(vmem_limit_bytes=4 * MIB),
        name="split_heads",
    )(hbm(x), hbm(cotangent))


def from_tokens(arrays, lists):
    num_tokens = lax.axis_size("tok")
    return tuple((d,) + pick((d, 0), lists) for d in range(1, num_tokens))


def small_kernel(gain_hbm, router_hbm, route_hbm, down_hbm, *refs):
    gain_ref, router_ref, chosen_ref, down_ref, routes, sems, down_sem = refs
    load = pltpu.make_async_copy(down_hbm.at[0, pl.ds(0, down_ref.shape[0])], down_ref, down_sem)
    load.start()
    copies = [
        pltpu.make_async_copy(src, dst, sems.at[i])
        for i, (src, dst) in enumerate(
            [
                (gain_hbm, gain_ref),
                (router_hbm, router_ref),
                (route_hbm, routes),
            ]
        )
    ]
    for copy in copies:
        copy.start()
    for copy in copies:
        copy.wait()
    rows, experts = chosen_ref.shape
    ids = lax.broadcasted_iota(jnp.int32, (experts, rows), 0)
    hit = routes[0:1, :] == ids
    for k in range(1, routes.shape[0]):
        hit = hit | (routes[k : k + 1, :] == ids)
    chosen_ref[...] = hit.astype(F32).T
    load.wait()


def small_operands(gain, router_rows, routes, w_down):
    experts, all_rows = 8, routes.shape[1]
    return pl.pallas_call(
        small_kernel,
        in_specs=[IN_HBM] * 4,
        out_specs=(IN_VMEM,) * 3 + (ANYWHERE,),
        out_shape=(
            jax.ShapeDtypeStruct(gain.shape, F32),
            jax.ShapeDtypeStruct(router_rows.shape, BF16),
            jax.ShapeDtypeStruct((all_rows, experts), F32),
            jax.ShapeDtypeStruct((w_down.shape[1] // 2,) + w_down.shape[2:], BF16),
        ),
        scratch_shapes=[
            pltpu.VMEM(routes.shape, jnp.int32),
            pltpu.SemaphoreType.DMA((3,)),
            pltpu.SemaphoreType.DMA(()),
        ],
        compiler_params=pltpu.CompilerParams(vmem_limit_bytes=4 * MIB),
        cost_estimate=pl.CostEstimate(flops=2**36, bytes_accessed=32 * MIB, transcendentals=0),
        name="small_operands",
    )(hbm(gain), hbm(router_rows), hbm(routes), hbm(w_down))


def norm_kernel(places, x_ref, gain_ref, *refs):
    heads, (normed_ref, summed_ref) = refs[:-2], refs[-2:]
    me = lax.axis_index("tok")
    width = heads[0].shape[2]
    own = head_slice(me, width)
    summed_ref[:, own] = 2.0 * x_ref[:, own].astype(F32)
    for d, i, j in places:
        place = head_slice(me ^ d, width)
        summed_ref[:, place] = x_ref[:, place].astype(F32) + heads[i][j].astype(F32)
    summed = summed_ref[...]
    inv_rms = lax.rsqrt(jnp.mean(summed * summed, axis=1, keepdims=True) + 1e-06)
    normed_ref[...] = (summed * inv_rms * gain_ref[...]).astype(BF16)


def norm_rows(x, gain, heads, places):
    return pl.pallas_call(
        functools.partial(norm_kernel, places),
        out_shape=(jax.ShapeDtypeStruct(x.shape, BF16), jax.ShapeDtypeStruct(x.shape, F32)),
        compiler_params=pltpu.CompilerParams(vmem_limit_bytes=4 * MIB),
        name="norm_rows",
    )(x, gain, *heads)


def join_kernel(*refs):
    assemble(refs[-1], refs[:-1])


def join_rows(chunks):
    rows, width = sum(chunk.shape[0] for chunk in chunks), chunks[0].shape[1]
    return pl.pallas_call(
        join_kernel,
        out_shape=jax.ShapeDtypeStruct((rows, width), BF16),
        compiler_params=pltpu.CompilerParams(vmem_limit_bytes=4 * MIB),
        name="join_rows",
    )(*chunks)


def load_weights(refs, place, experts, sems):
    copies = []
    for i, (e, ref) in enumerate((e, ref) for e in experts for ref in refs):
        hidden = ref.shape[3]
        columns = pl.ds(i * hidden, hidden)
        copies.append(pltpu.make_async_copy(ref.at[0, e], place.at[:, columns], sems.at[i]))
        copies[-1].start()
    return copies


def back_kernel(count, *refs):
    chunks, (first, down_hbm, gate_hbm, up_hbm, back_ref, weights_ref) = refs[:count], refs[count : count + 6]
    cot, second, down_sems, sems = refs[count + 6 :]
    split = first.shape[0]
    experts = split + second.shape[0]
    copies = [
        pltpu.make_async_copy(down_hbm.at[0, split + e], second.at[e], down_sems.at[e])
        for e in range(experts - split)
    ]
    for copy in copies:
        copy.start()
    loads = load_weights((gate_hbm, up_hbm), weights_ref, range(experts // 2), sems)
    assemble(cot, chunks)
    for e in range(split):
        back_ref[e] = dot(cot[...], first[e], NT)
    for e, copy in enumerate(copies):
        copy.wait()
        back_ref[split + e] = dot(cot[...], second[e], NT)
    for load in loads:
        load.wait()


def back_hidden(chunks, first, w_down, w_gate, w_up):
    _, experts, hidden, width = w_down.shape
    rows = sum(chunk.shape[0] for chunk in chunks)
    rest = experts - first.shape[0]
    return pl.pallas_call(
        functools.partial(back_kernel, len(chunks)),
        in_specs=[IN_VMEM] * (len(chunks) + 1) + [IN_HBM] * 3,
        out_specs=(IN_VMEM, ANYWHERE),
        out_shape=(
            jax.ShapeDtypeStruct((experts, rows, hidden), F32),
            jax.ShapeDtypeStruct((width, experts // 2 * 2 * hidden), BF16),
        ),
        scratch_shapes=[
            pltpu.VMEM((rows, width), BF16),
            pltpu.VMEM((rest, hidden, width), BF16),
            pltpu.SemaphoreType.DMA((rest,)),
            pltpu.SemaphoreType.DMA((experts // 2 * 2,)),
        ],
        compiler_params=pltpu.CompilerParams(vmem_limit_bytes=16 * MIB),
        cost_estimate=pl.CostEstimate(
            flops=0,
            bytes_accessed=0,
            transcendentals=0,
        ),
        name="back_hidden",
    )(*chunks, vmem(first), hbm(w_down), hbm(w_gate), hbm(w_up))


def expert_kernel(size, *refs):
    chunks, (first, gate_hbm, up_hbm, back_ref) = refs[:size], refs[size : size + 4]
    chosen_ref, router_ref, gain_ref, grads_out, act_out, sent_out = refs[size + 4 : size + 10]
    kept, (small_out, normed, second, sems) = refs[size + 10 : -4], refs[-4:]
    own, width = chunks[0].shape
    experts = router_ref.shape[0]
    hidden = back_ref.shape[2]
    split = experts // 2
    loads = load_weights((gate_hbm, up_hbm), second, range(split, experts), sems)
    assemble(normed, chunks)
    me = lax.axis_index("dp")
    hits = []
    for i in range(size):
        start = pl.multiple_of((me ^ device_of(i, size)) * own, own)
        hits.append(chosen_ref[pl.ds(start, own), :experts])
    chosen = jnp.concatenate(hits, axis=0)
    prob = jax.nn.sigmoid(dot(normed[...], router_ref[...], NT))
    gates = prob * chosen

    def forward(e):
        if e < split:
            return dot(normed[...], first[:, 2 * e * hidden : 2 * (e + 1) * hidden], NN)
        e -= split
        loads[2 * e].wait()
        loads[2 * e + 1].wait()
        return dot(normed[...], second[:, 2 * e * hidden : 2 * (e + 1) * hidden], NN)

    shares = []
    later = forward(0)
    for e in range(experts):
        pre_gate, pre_up = later[:, :hidden], later[:, hidden:]
        if e + 1 < experts:
            later = forward(e + 1)
        gate = gates[:, e : e + 1]
        back = back_ref[e]
        sigma = jax.nn.sigmoid(pre_gate)
        silu = pre_gate * sigma
        act = silu * pre_up
        shares.append(jnp.sum(act * back, axis=1, keepdims=True))
        scaled = gate * back
        grad_gate = scaled * pre_up * (sigma * (1.0 + pre_gate * (1.0 - sigma)))
        grads_out[:, 2 * e * hidden : (2 * e + 1) * hidden] = grad_gate.astype(BF16)
        grads_out[:, (2 * e + 1) * hidden : (2 * e + 2) * hidden] = (scaled * silu).astype(BF16)
        act_out[:, e * hidden : (e + 1) * hidden] = (gate * act).astype(BF16)
    coef = jnp.concatenate(shares, axis=1) * gates * (1.0 - prob)
    high = coef.astype(BF16).astype(F32)
    middle = (coef - high).astype(BF16).astype(F32)
    low = coef - high - middle
    terms = jnp.concatenate([high, middle, low], axis=1).astype(BF16)
    router = router_ref[...].astype(F32)
    router = jnp.concatenate([router] * 3, axis=0).astype(BF16)
    small = dot(terms, normed[...], TN)
    small_out[:experts] = small[:experts] + small[experts : 2 * experts] + small[2 * experts :]
    half = size // 2 * own
    step = width // 4
    for c in range(0, width, step):
        here = slice(c, c + step)
        grad = dot(grads_out[:, : 2 * split * hidden], first[here, :], NT)
        grad = grad + dot(grads_out[:, 2 * split * hidden :], second[here, :], NT)
        grad = grad + dot(terms, router[:, here], NN)
        rows_here = normed[:, here].astype(F32)
        gain = jnp.sum(grad * rows_here, axis=0, keepdims=True) / gain_ref[:, here]
        small_out[experts:, here] = jnp.broadcast_to(gain, (8 - experts, step))
        grad = grad.astype(BF16)
        for i in range(size // 2):
            kept[i][:, here] = grad[i * own : (i + 1) * own]
        sent_out[:half, here] = grad[half:]
    core = me % 2
    sent_out[half:] = two_terms(small_out[:, head_slice(1 - core, width // 2)])


def experts_backward(chunks, first, w_gate, w_up, back, chosen, router_rows, gain):
    size = len(chunks)
    own, width = chunks[0].shape
    experts, rows, hidden = back.shape
    kept = jax.ShapeDtypeStruct((own, width), BF16)
    return pl.pallas_call(
        functools.partial(expert_kernel, size),
        in_specs=[IN_VMEM] * (size + 1) + [IN_HBM] * 2 + [IN_VMEM] * 4,
        out_shape=(
            jax.ShapeDtypeStruct((rows, 2 * experts * hidden), BF16),
            jax.ShapeDtypeStruct((rows, experts * hidden), BF16),
            jax.ShapeDtypeStruct((rows // 2 + 8, width), BF16),
        )
        + (kept,) * (size // 2)
        + (jax.ShapeDtypeStruct((8, width), F32),),
        scratch_shapes=[
            pltpu.VMEM((rows, width), BF16),
            pltpu.VMEM((width, 2 * (experts - experts // 2) * hidden), BF16),
            pltpu.SemaphoreType.DMA((2 * (experts - experts // 2),)),
        ],
        compiler_params=pltpu.CompilerParams(vmem_limit_bytes=20 * MIB),
        cost_estimate=pl.CostEstimate(
            flops=8 * experts * rows * hidden * width,
            bytes_accessed=experts * hidden * (width * 4 + rows * 10) + rows * width * 4,
            transcendentals=experts * rows * hidden,
        ),
        name="experts_backward",
    )(*chunks, vmem(first), hbm(w_gate), hbm(w_up), back, chosen, router_rows, gain)


def two_terms(small):
    high = small.astype(BF16)
    low = (small - high.astype(F32)).astype(BF16)
    return jnp.concatenate([high, low], axis=1)


def one_term(terms):
    half = terms.shape[1] // 2
    return terms[:, :half].astype(F32) + terms[:, half:].astype(F32)


def pair_kernel(count, *refs):
    kept, (arrived_ref, small_ref), outs = refs[:count], refs[count : count + 2], refs[count + 2 :]
    own, width = kept[0].shape
    core = lax.axis_index("dp") % 2
    mine = small_ref[:, head_slice(core, width // 2)]
    small = two_terms(mine + one_term(arrived_ref[count * own :]))
    for i in range(count):
        arrived = arrived_ref[i * own : (i + 1) * own].astype(F32)
        outs[i][:own] = (kept[i][...].astype(F32) + arrived).astype(BF16)
        outs[i][own:] = small


def pair_sum(kept, arrived, small):
    own, width = kept[0].shape
    return pl.pallas_call(
        functools.partial(pair_kernel, len(kept)),
        out_shape=(jax.ShapeDtypeStruct((own + 8, width), BF16),) * len(kept),
        compiler_params=pltpu.CompilerParams(vmem_limit_bytes=4 * MIB),
        name="pair_sum",
    )(*kept, arrived, small)


SLOTS = 4
DOWN_MIDDLE = 2


def write_out(tiles, buffers, sems):
    copies = []
    for i, (value, destination) in enumerate(tiles):
        slot = i % SLOTS
        if i >= SLOTS:
            copies[i - SLOTS].wait()
        rows, columns = destination.shape
        buffer = next(ref for ref in buffers if ref.shape[2] == columns and ref.shape[1] >= rows)
        place = buffer.at[slot, pl.ds(0, rows)]
        place[...] = value().astype(BF16)
        copies.append(pltpu.make_async_copy(place, destination, sems.at[slot]))
        copies[-1].start()
    for copy in copies[-SLOTS:]:
        copy.wait()


def weight_kernel(counts, down_experts, *refs):
    normed_chunks, refs = refs[: counts[0]], refs[counts[0] :]
    cot_chunks, refs = refs[: counts[1]], refs[counts[1] :]
    buffers, sems = refs[-3:-1], refs[-1]
    tiles = []
    if counts[0]:
        grads_ref, act_ref = refs[:2]
        gate_out, up_out, down_out, normed, cot = refs[-8:-3]
        assemble(normed, normed_chunks)
        hidden = gate_out.shape[3]
        for e in range(gate_out.shape[1]):
            for i, out in enumerate((gate_out, up_out)):
                first = (2 * e + i) * hidden
                columns = slice(first, first + hidden)
                value = lambda columns=columns: dot(normed[...], grads_ref[:, columns], TN)
                tiles.append((value, out.at[0, e]))
    else:
        act_ref = refs[0]
        down_out, cot = refs[-5:-3]
    assemble(cot, cot_chunks)
    hidden = down_out.shape[2]
    for e in down_experts:
        parts = 2 if e == down_experts[-1] else 1
        step = hidden // parts
        for first in range(0, hidden, step):
            columns = slice(e * hidden + first, e * hidden + first + step)
            value = lambda columns=columns: dot(act_ref[:, columns], cot[...], TN)
            tiles.append((value, down_out.at[0, e, pl.ds(first, step)]))
    write_out(tiles, buffers, sems)


def weight_gradients(cot_chunks, act, down_shape, down_experts, name, started=None, gate_up=None):
    width = cot_chunks[0].shape[1]
    rows = act.shape[0]
    normed_chunks, grads, shapes = gate_up or ([], None, [])
    operands = [*normed_chunks, *cot_chunks, *([grads] if gate_up else []), act]
    specs = [IN_VMEM] * len(operands)
    if started is not None:
        operands, specs = operands + [started], specs + [IN_HBM]
    shapes = [*shapes, down_shape]
    tile = down_shape[2] * width
    flops = 2 * rows * (tile * len(down_experts) + sum(math.prod(shape) for shape in shapes[:-1]))
    slot = (down_shape[2], width)
    return pl.pallas_call(
        functools.partial(weight_kernel, (len(normed_chunks), len(cot_chunks)), down_experts),
        in_specs=specs,
        out_specs=(IN_HBM,) * len(shapes),
        out_shape=tuple(jax.ShapeDtypeStruct(shape, BF16) for shape in shapes),
        input_output_aliases={} if started is None else {len(operands) - 1: len(shapes) - 1},
        scratch_shapes=[pltpu.VMEM((rows, width), BF16)] * (2 if gate_up else 1)
        + [pltpu.VMEM((SLOTS,) + (slot[::-1] if gate_up else (16, 128)), BF16)]
        + [pltpu.VMEM((SLOTS,) + slot, BF16)]
        + [pltpu.SemaphoreType.DMA((SLOTS,))],
        compiler_params=pltpu.CompilerParams(vmem_limit_bytes=24 * MIB),
        cost_estimate=pl.CostEstimate(flops=flops, bytes_accessed=flops // rows, transcendentals=0),
        name=name,
    )(*operands)


def norm_back_kernel(count, *refs):
    parts, (summed_ref, gain_ref, cot_ref) = refs[:count], refs[count : count + 3]
    grad_ref, small_out, *sends = refs[count + 3 :]
    own = summed_ref.shape[0]
    grad_normed = parts[0][:own].astype(F32)
    for part in parts[1:]:
        grad_normed = grad_normed + part[:own].astype(F32)
    summed = summed_ref[...]
    inv_rms = lax.rsqrt(jnp.mean(summed * summed, axis=1, keepdims=True) + 1e-06)
    scaled = grad_normed * gain_ref[...]
    centre = jnp.mean(scaled * summed, axis=1, keepdims=True)
    grad = inv_rms * scaled - summed * (inv_rms * inv_rms * inv_rms * centre)
    grad_ref[...] = grad + cot_ref[...].astype(F32)
    head = sends[0].shape[2]
    for s, send in enumerate(sends):
        place = head_slice(lax.axis_index("tok") ^ (s + 1), head)
        send[0] = grad_ref[:, place].astype(BF16)
    me = lax.axis_index("dp") // 2
    smalls = jnp.stack([one_term(part[own:]) for part in parts])
    small = jnp.zeros(smalls.shape[1:], F32)
    for chip in range(count):
        for i in range(count):
            small = small + jnp.where((me ^ i) == chip, smalls[i], 0.0)
    small_out[...] = small


def norm_backward(parts, summed, gain, cot):
    rows, width = summed.shape
    num_tokens = lax.axis_size("tok")
    head = jax.ShapeDtypeStruct((1, rows, width // num_tokens), BF16)
    return pl.pallas_call(
        functools.partial(norm_back_kernel, len(parts)),
        out_shape=(
            jax.ShapeDtypeStruct((rows, width), F32),
            jax.ShapeDtypeStruct((8, width // 2), F32),
        )
        + (head,) * (num_tokens - 1),
        compiler_params=pltpu.CompilerParams(vmem_limit_bytes=4 * MIB),
        name="norm_backward",
    )(*parts, summed, gain, cot)


def finish_kernel(places, grad_ref, small_ref, other_ref, *refs):
    heads, (out_ref, router_out, gain_out) = refs[:-3], refs[-3:]
    core = lax.axis_index("dp") % 2
    experts, columns = router_out.shape
    for ref, c in ((small_ref, core), (other_ref, 1 - core)):
        place = head_slice(c, columns // 2)
        router_out[:, place] = ref[:experts]
        gain_out[:, place] = ref[experts : experts + 1]
    me = lax.axis_index("tok")
    width = heads[0].shape[2]
    own = head_slice(me, width)
    out_ref[0, :, own] = (2.0 * grad_ref[:, own]).astype(BF16)
    for d, i, j in places:
        place = head_slice(me ^ d, width)
        out_ref[0, :, place] = (grad_ref[:, place] + heads[i][j].astype(F32)).astype(BF16)


def finish(grad_summed, heads, places, small, other, experts):
    rows, width = grad_summed.shape
    return pl.pallas_call(
        functools.partial(finish_kernel, places),
        out_shape=(
            jax.ShapeDtypeStruct((1, rows, width), BF16),
            jax.ShapeDtypeStruct((experts, width), F32),
            jax.ShapeDtypeStruct((1, width), F32),
        ),
        compiler_params=pltpu.CompilerParams(vmem_limit_bytes=4 * MIB),
        name="finish",
    )(grad_summed, small, other, *heads)


def shards(inputs, cotangent, norm_gain, router_weight, route_ids, w_gate, w_up, w_down):
    width = inputs.shape[2]
    size = lax.axis_size("dp")
    experts = w_gate.shape[1]

    x, cot, first, kept = split_heads(inputs, cotangent)
    heads, items = first_stage(first, kept)
    heads, items = other_stages(heads, items)
    cots = gather_chips(cot)
    norm_gain, heads[1] = after((norm_gain, heads[1]))
    gain, router_rows, chosen, down = small_operands(
        norm_gain, router_weight[0].T, route_ids[0].T, w_down
    )
    heads, gain, router_rows, chosen, down = after((heads, gain, router_rows, chosen, down))
    places = from_tokens(heads, items)
    normed, summed = norm_rows(x, gain, heads, places)
    far_rows = gather_chips(normed)
    cots, summed = after((cots, summed))
    cots = gather_cores([join_rows(cots)])
    back, weights = back_hidden(cots, down, w_down, w_gate, w_up)
    far_rows[1:], back = after((far_rows[1:], back))
    rows = gather_cores(far_rows)
    grads, act, sent, *kept, small = experts_backward(
        rows, weights, w_gate, w_up, back, chosen, router_rows, gain
    )
    sent, act = after((sent, act))
    arrived = exchange(sent, "dp", 1)
    (grad_down,) = weight_gradients(cots, act, w_down.shape, range(1), "grad_down_0")
    arrived, grad_down, grads = after((arrived, grad_down, grads))
    pairs = pair_sum(kept, arrived, small)
    pairs, grads = after((pairs, grads))
    far = [exchange(pairs[s], "dp", 2 * s) for s in reversed(range(1, size // 2))]
    grad_gate, grad_up, grad_down = weight_gradients(
        cots,
        act,
        w_down.shape,
        range(1, DOWN_MIDDLE),
        "grad_gate_up",
        grad_down,
        (rows, grads, (w_gate.shape, w_up.shape)),
    )
    far, grad_gate, grad_up, grad_down = after((far, grad_gate, grad_up, grad_down))
    grad_summed, small, *sends = norm_backward([pairs[0]] + far[::-1], summed, gain, cot)
    sends, act, small = after((sends, act, small))
    other = exchange(small, "dp", 1)
    returned = [exchange(send, "tok", s + 1) for s, send in reversed(list(enumerate(sends)))]
    (grad_down,) = weight_gradients(
        cots, act, w_down.shape, range(DOWN_MIDDLE, experts), "grad_down", grad_down
    )
    returned, grad_down, other = after((returned, grad_down, other))
    places = tuple((len(returned) - s, s, 0) for s in range(len(returned)))
    grad_inputs, grad_router, grad_gain = finish(grad_summed, returned, places, small, other, experts)
    return (
        grad_inputs,
        grad_gate,
        grad_up,
        grad_down,
        grad_router.T[None],
        grad_gain,
    )


def solution(mesh):
    return jax.shard_map(
        shards,
        mesh=mesh,
        in_specs=(
            P("tok", "dp", None),
            P("tok", "dp", None),
            P("tok", None),
            P("tok", None, None),
            P("tok", None, None),
            P("tok", None, None, "dp"),
            P("tok", None, None, "dp"),
            P("tok", None, "dp", None),
        ),
        out_specs=(
            P("tok", "dp", None),
            P("tok", None, None, "dp"),
            P("tok", None, None, "dp"),
            P("tok", None, "dp", None),
            P("tok", None, None),
            P("tok", None),
        ),
        check_vma=False,
    )
```

```python
import functools
import math

import jax
import jax.numpy as jnp
from jax import lax
from jax.experimental import pallas as pl
from jax.experimental.pallas import tpu as pltpu
from jax.sharding import PartitionSpec as P

BF16 = jnp.bfloat16
F32 = jnp.float32
MIB = 1024 * 1024


def dot(left, right, dims):
    return lax.dot_general(left, right, (dims, ((), ())), preferred_element_type=F32)


NN = ((1,), (0,))
NT = ((1,), (1,))
TN = ((0,), (0,))


def exchange(value, axis, distance):
    size = lax.axis_size(axis)
    return lax.ppermute(value, axis, [(i, i ^ distance) for i in range(size)])


def gather_chips(rows):
    size = lax.axis_size("dp")
    return [rows] + [exchange(rows, "dp", s) for s in range(2, size, 2)]


def gather_cores(chunks):
    return list(chunks) + [exchange(chunk, "dp", 1) for chunk in chunks]


def after(values):
    return lax.optimization_barrier(values)


def device_of(block, size):
    return 2 * block if block < size // 2 else 2 * block + 1 - size


def assemble(rows, chunks):
    first = 0
    for chunk in chunks:
        rows[first : first + chunk.shape[0]] = chunk[...]
        first += chunk.shape[0]


def head_slice(slot, width):
    return pl.ds(pl.multiple_of(slot * width, width), width)


def hbm(array):
    return pltpu.with_memory_space_constraint(array, pltpu.HBM)


def vmem(array):
    return pltpu.with_memory_space_constraint(array, pltpu.VMEM)


IN_HBM = pl.BlockSpec(memory_space=pltpu.HBM)
IN_VMEM = pl.BlockSpec(memory_space=pltpu.VMEM)
ANYWHERE = pl.BlockSpec(memory_space=pl.ANY)


def head_plan(num_tokens):
    held, stages, bit = [(0, d) for d in range(1, num_tokens)], [], 1
    while bit < num_tokens:
        sent = [item for item in held if item[1] & bit]
        received = [(source ^ bit, target ^ bit) for source, target in sent]
        held = [item for item in held if not item[1] & bit] + received
        stages.append((bit, sent, received))
        bit *= 2
    first = stages[0][1]
    return first, [(0, d) for d in range(1, num_tokens) if (0, d) not in first], stages


def pick(item, lists):
    for i, items in enumerate(lists):
        if item in items:
            return i, items.index(item)


def pack_kernel(picks, *refs):
    for k, (i, j) in enumerate(picks):
        refs[-1][k] = refs[i][j]


def pack_heads(arrays, picks):
    return pl.pallas_call(
        functools.partial(pack_kernel, picks),
        out_shape=jax.ShapeDtypeStruct((len(picks),) + arrays[0].shape[1:], BF16),
        compiler_params=pltpu.CompilerParams(vmem_limit_bytes=4 * MIB),
        name="pack_heads",
    )(*arrays)


def first_stage(first, kept):
    _, kept_items, stages = head_plan(lax.axis_size("tok"))
    bit, _, received = stages[0]
    return [kept, exchange(first, "tok", bit)], [kept_items, received]


def other_stages(arrays, lists):
    for bit, sent, received in head_plan(lax.axis_size("tok"))[2][1:]:
        payload = pack_heads(arrays, [pick(item, lists) for item in sent])
        arrays = arrays + [exchange(payload, "tok", bit)]
        lists = lists + [received]
    return arrays, lists


def heads_kernel(x_hbm, cot_hbm, x_ref, cot_ref, first_ref, kept_ref, sems):
    copy_x = pltpu.make_async_copy(x_hbm.at[0], x_ref, sems.at[0])
    copy_cot = pltpu.make_async_copy(cot_hbm.at[0], cot_ref, sems.at[1])
    copy_x.start()
    copy_cot.start()
    copy_x.wait()
    store_heads(x_ref, first_ref, kept_ref)
    copy_cot.wait()


def store_heads(rows_ref, first_ref, kept_ref):
    width = first_ref.shape[2]
    first, kept, _ = head_plan(rows_ref.shape[1] // width)
    me = lax.axis_index("tok")
    for ref, items in ((first_ref, first), (kept_ref, kept)):
        for k, (_, d) in enumerate(items):
            ref[k] = rows_ref[:, head_slice(me ^ d, width)].astype(BF16)


def head_shapes(rows, width):
    num_tokens = lax.axis_size("tok")
    first, kept, _ = head_plan(num_tokens)
    return tuple(
        jax.ShapeDtypeStruct((len(items), rows, width // num_tokens), BF16) for items in (first, kept)
    )


def split_heads(x, cotangent):
    _, rows, width = x.shape
    return pl.pallas_call(
        heads_kernel,
        in_specs=[IN_HBM] * 2,
        out_shape=(jax.ShapeDtypeStruct((rows, width), BF16),) * 2 + head_shapes(rows, width),
        scratch_shapes=[pltpu.SemaphoreType.DMA((2,))],
        compiler_params=pltpu.CompilerParams(vmem_limit_bytes=4 * MIB),
        name="split_heads",
    )(hbm(x), hbm(cotangent))


def from_tokens(arrays, lists):
    num_tokens = lax.axis_size("tok")
    return tuple((d,) + pick((d, 0), lists) for d in range(1, num_tokens))


def small_kernel(gain_hbm, router_hbm, route_hbm, down_hbm, *refs):
    gain_ref, router_ref, chosen_ref, down_ref, routes, sems, down_sem = refs
    load = pltpu.make_async_copy(down_hbm.at[0, pl.ds(0, down_ref.shape[0])], down_ref, down_sem)
    load.start()
    copies = [
        pltpu.make_async_copy(src, dst, sems.at[i])
        for i, (src, dst) in enumerate(
            [
                (gain_hbm, gain_ref),
                (router_hbm, router_ref),
                (route_hbm, routes),
            ]
        )
    ]
    for copy in copies:
        copy.start()
    for copy in copies:
        copy.wait()
    rows, experts = chosen_ref.shape
    ids = lax.broadcasted_iota(jnp.int32, (experts, rows), 0)
    hit = routes[0:1, :] == ids
    for k in range(1, routes.shape[0]):
        hit = hit | (routes[k : k + 1, :] == ids)
    chosen_ref[...] = hit.astype(F32).T
    load.wait()


def small_operands(gain, router_rows, routes, w_down):
    experts, all_rows = 8, routes.shape[1]
    return pl.pallas_call(
        small_kernel,
        in_specs=[IN_HBM] * 4,
        out_specs=(IN_VMEM,) * 3 + (ANYWHERE,),
        out_shape=(
            jax.ShapeDtypeStruct(gain.shape, F32),
            jax.ShapeDtypeStruct(router_rows.shape, BF16),
            jax.ShapeDtypeStruct((all_rows, experts), F32),
            jax.ShapeDtypeStruct((w_down.shape[1] - 1,) + w_down.shape[2:], BF16),
        ),
        scratch_shapes=[
            pltpu.VMEM(routes.shape, jnp.int32),
            pltpu.SemaphoreType.DMA((3,)),
            pltpu.SemaphoreType.DMA(()),
        ],
        compiler_params=pltpu.CompilerParams(vmem_limit_bytes=4 * MIB),
        cost_estimate=pl.CostEstimate(flops=2**36, bytes_accessed=32 * MIB, transcendentals=0),
        name="small_operands",
    )(hbm(gain), hbm(router_rows), hbm(routes), hbm(w_down))


def norm_kernel(places, x_ref, gain_ref, *refs):
    heads, (normed_ref, summed_ref) = refs[:-2], refs[-2:]
    me = lax.axis_index("tok")
    width = heads[0].shape[2]
    own = head_slice(me, width)
    summed_ref[:, own] = 2.0 * x_ref[:, own].astype(F32)
    for d, i, j in places:
        place = head_slice(me ^ d, width)
        summed_ref[:, place] = x_ref[:, place].astype(F32) + heads[i][j].astype(F32)
    summed = summed_ref[...]
    inv_rms = lax.rsqrt(jnp.mean(summed * summed, axis=1, keepdims=True) + 1e-06)
    normed_ref[...] = (summed * inv_rms * gain_ref[...]).astype(BF16)


def norm_rows(x, gain, heads, places):
    return pl.pallas_call(
        functools.partial(norm_kernel, places),
        out_shape=(jax.ShapeDtypeStruct(x.shape, BF16), jax.ShapeDtypeStruct(x.shape, F32)),
        compiler_params=pltpu.CompilerParams(vmem_limit_bytes=4 * MIB),
        name="norm_rows",
    )(x, gain, *heads)


def join_kernel(*refs):
    assemble(refs[-1], refs[:-1])


def join_rows(chunks):
    rows, width = sum(chunk.shape[0] for chunk in chunks), chunks[0].shape[1]
    return pl.pallas_call(
        join_kernel,
        out_shape=jax.ShapeDtypeStruct((rows, width), BF16),
        compiler_params=pltpu.CompilerParams(vmem_limit_bytes=4 * MIB),
        name="join_rows",
    )(*chunks)


def load_weights(refs, place, experts, sems, start=0):
    copies = []
    for i, (e, ref) in enumerate((e, ref) for e in experts for ref in refs):
        hidden = ref.shape[3]
        columns = pl.ds((2 * start + i) * hidden, hidden)
        copies.append(pltpu.make_async_copy(ref.at[0, e], place.at[:, columns], sems.at[i]))
        copies[-1].start()
    return copies


def load_kernel(gate_hbm, up_hbm, weights_ref, sems):
    for load in load_weights((gate_hbm, up_hbm), weights_ref, range(1), sems):
        load.wait()


def load_first(w_gate, w_up):
    _, experts, width, hidden = w_gate.shape
    return pl.pallas_call(
        load_kernel,
        in_specs=[IN_HBM] * 2,
        out_specs=ANYWHERE,
        out_shape=jax.ShapeDtypeStruct((width, experts // 2 * 2 * hidden), BF16),
        scratch_shapes=[pltpu.SemaphoreType.DMA((2,))],
        compiler_params=pltpu.CompilerParams(vmem_limit_bytes=1 * MIB),
        cost_estimate=pl.CostEstimate(flops=2**36, bytes_accessed=4 * width * hidden, transcendentals=0),
        name="load_first",
    )(hbm(w_gate), hbm(w_up))


def back_kernel(count, *refs):
    chunks, (first, down_hbm, gate_hbm, up_hbm, _, back_ref, weights_ref) = refs[:count], refs[count : count + 7]
    cot, second, down_sems, sems = refs[count + 7 :]
    split = first.shape[0]
    experts = split + second.shape[0]
    copies = [
        pltpu.make_async_copy(down_hbm.at[0, split + e], second.at[e], down_sems.at[e])
        for e in range(experts - split)
    ]
    for copy in copies:
        copy.start()
    loads = load_weights((gate_hbm, up_hbm), weights_ref, range(1, experts // 2), sems, 1)
    assemble(cot, chunks)
    for e in range(split):
        back_ref[e] = dot(cot[...], first[e], NT)
    for e, copy in enumerate(copies):
        copy.wait()
        back_ref[split + e] = dot(cot[...], second[e], NT)
    for load in loads:
        load.wait()


def back_hidden(chunks, first, w_down, w_gate, w_up, weights):
    _, experts, hidden, width = w_down.shape
    rows = sum(chunk.shape[0] for chunk in chunks)
    rest = experts - first.shape[0]
    return pl.pallas_call(
        functools.partial(back_kernel, len(chunks)),
        in_specs=[IN_VMEM] * (len(chunks) + 1) + [IN_HBM] * 3 + [ANYWHERE],
        input_output_aliases={len(chunks) + 4: 1},
        out_specs=(IN_VMEM, ANYWHERE),
        out_shape=(
            jax.ShapeDtypeStruct((experts, rows, hidden), F32),
            jax.ShapeDtypeStruct((width, experts // 2 * 2 * hidden), BF16),
        ),
        scratch_shapes=[
            pltpu.VMEM((rows, width), BF16),
            pltpu.VMEM((rest, hidden, width), BF16),
            pltpu.SemaphoreType.DMA((rest,)),
            pltpu.SemaphoreType.DMA(((experts // 2 - 1) * 2,)),
        ],
        compiler_params=pltpu.CompilerParams(vmem_limit_bytes=16 * MIB),
        cost_estimate=pl.CostEstimate(
            flops=0,
            bytes_accessed=0,
            transcendentals=0,
        ),
        name="back_hidden",
    )(*chunks, vmem(first), hbm(w_down), hbm(w_gate), hbm(w_up), weights)


def expert_kernel(size, *refs):
    chunks, (first, gate_hbm, up_hbm, back_ref) = refs[:size], refs[size : size + 4]
    chosen_ref, router_ref, gain_ref, grads_out, act_out, sent_out = refs[size + 4 : size + 10]
    kept, (small_out, normed, total, second, sems) = refs[size + 10 : -5], refs[-5:]
    own, width = chunks[0].shape
    experts = router_ref.shape[0]
    hidden = back_ref.shape[2]
    split = experts // 2
    loads = load_weights((gate_hbm, up_hbm), second, range(split, experts), sems)
    assemble(normed, chunks)
    me = lax.axis_index("dp")
    hits = []
    for i in range(size):
        start = pl.multiple_of((me ^ device_of(i, size)) * own, own)
        hits.append(chosen_ref[pl.ds(start, own), :experts])
    chosen = jnp.concatenate(hits, axis=0)
    prob = jax.nn.sigmoid(dot(normed[...], router_ref[...], NT))
    gates = prob * chosen

    def forward(e):
        if e < split:
            return dot(normed[...], first[:, 2 * e * hidden : 2 * (e + 1) * hidden], NN)
        e -= split
        loads[2 * e].wait()
        loads[2 * e + 1].wait()
        return dot(normed[...], second[:, 2 * e * hidden : 2 * (e + 1) * hidden], NN)

    shares = []
    later = forward(0)
    for e in range(experts):
        pre_gate, pre_up = later[:, :hidden], later[:, hidden:]
        if e + 1 < experts:
            later = forward(e + 1)
        gate = gates[:, e : e + 1]
        back = back_ref[e]
        sigma = jax.nn.sigmoid(pre_gate)
        silu = pre_gate * sigma
        act = silu * pre_up
        shares.append(jnp.sum(act * back, axis=1, keepdims=True))
        scaled = gate * back
        grad_gate = scaled * pre_up * (sigma * (1.0 + pre_gate * (1.0 - sigma)))
        grads_out[:, 2 * e * hidden : (2 * e + 1) * hidden] = grad_gate.astype(BF16)
        grads_out[:, (2 * e + 1) * hidden : (2 * e + 2) * hidden] = (scaled * silu).astype(BF16)
        act_out[:, e * hidden : (e + 1) * hidden] = (gate * act).astype(BF16)
        if e == experts - 2:
            total[...] = dot(grads_out[:, : 2 * split * hidden], first[...], NT)
    coef = jnp.concatenate(shares, axis=1) * gates * (1.0 - prob)
    high = coef.astype(BF16).astype(F32)
    middle = (coef - high).astype(BF16).astype(F32)
    low = coef - high - middle
    terms = jnp.concatenate([high, middle, low], axis=1).astype(BF16)
    router = router_ref[...].astype(F32)
    router = jnp.concatenate([router] * 3, axis=0).astype(BF16)
    small = dot(terms, normed[...], TN)
    small_out[:experts] = small[:experts] + small[experts : 2 * experts] + small[2 * experts :]
    half = size // 2 * own
    step = width // 4
    for c in range(0, width, step):
        here = slice(c, c + step)
        grad = total[:, here] + dot(grads_out[:, 2 * split * hidden :], second[here, :], NT)
        grad = grad + dot(terms, router[:, here], NN)
        rows_here = normed[:, here].astype(F32)
        gain = jnp.sum(grad * rows_here, axis=0, keepdims=True) / gain_ref[:, here]
        small_out[experts:, here] = jnp.broadcast_to(gain, (8 - experts, step))
        grad = grad.astype(BF16)
        for i in range(size // 2):
            kept[i][:, here] = grad[i * own : (i + 1) * own]
        sent_out[:half, here] = grad[half:]
    core = me % 2
    sent_out[half:] = two_terms(small_out[:, head_slice(1 - core, width // 2)])


def experts_backward(chunks, first, w_gate, w_up, back, chosen, router_rows, gain):
    size = len(chunks)
    own, width = chunks[0].shape
    experts, rows, hidden = back.shape
    kept = jax.ShapeDtypeStruct((own, width), BF16)
    return pl.pallas_call(
        functools.partial(expert_kernel, size),
        in_specs=[IN_VMEM] * (size + 1) + [IN_HBM] * 2 + [IN_VMEM] * 4,
        out_shape=(
            jax.ShapeDtypeStruct((rows, 2 * experts * hidden), BF16),
            jax.ShapeDtypeStruct((rows, experts * hidden), BF16),
            jax.ShapeDtypeStruct((rows // 2 + 8, width), BF16),
        )
        + (kept,) * (size // 2)
        + (jax.ShapeDtypeStruct((8, width), F32),),
        scratch_shapes=[
            pltpu.VMEM((rows, width), BF16),
            pltpu.VMEM((rows, width), F32),
            pltpu.VMEM((width, 2 * (experts - experts // 2) * hidden), BF16),
            pltpu.SemaphoreType.DMA((2 * (experts - experts // 2),)),
        ],
        compiler_params=pltpu.CompilerParams(vmem_limit_bytes=20 * MIB),
        cost_estimate=pl.CostEstimate(
            flops=8 * experts * rows * hidden * width,
            bytes_accessed=experts * hidden * (width * 4 + rows * 10) + rows * width * 4,
            transcendentals=experts * rows * hidden,
        ),
        name="experts_backward",
    )(*chunks, vmem(first), hbm(w_gate), hbm(w_up), back, chosen, router_rows, gain)


def two_terms(small):
    high = small.astype(BF16)
    low = (small - high.astype(F32)).astype(BF16)
    return jnp.concatenate([high, low], axis=1)


def one_term(terms):
    half = terms.shape[1] // 2
    return terms[:, :half].astype(F32) + terms[:, half:].astype(F32)


def pair_kernel(count, *refs):
    kept, (arrived_ref, small_ref), outs = refs[:count], refs[count : count + 2], refs[count + 2 :]
    own, width = kept[0].shape
    core = lax.axis_index("dp") % 2
    mine = small_ref[:, head_slice(core, width // 2)]
    small = two_terms(mine + one_term(arrived_ref[count * own :]))
    for i in range(count):
        arrived = arrived_ref[i * own : (i + 1) * own].astype(F32)
        outs[i][:own] = (kept[i][...].astype(F32) + arrived).astype(BF16)
        outs[i][own:] = small


def pair_sum(kept, arrived, small):
    own, width = kept[0].shape
    return pl.pallas_call(
        functools.partial(pair_kernel, len(kept)),
        out_shape=(jax.ShapeDtypeStruct((own + 8, width), BF16),) * len(kept),
        compiler_params=pltpu.CompilerParams(vmem_limit_bytes=4 * MIB),
        name="pair_sum",
    )(*kept, arrived, small)


SLOTS = 4
DOWN_MIDDLE = 2


def write_out(tiles, buffers, sems):
    copies = []
    for i, (value, destination) in enumerate(tiles):
        slot = i % SLOTS
        if i >= SLOTS:
            copies[i - SLOTS].wait()
        rows, columns = destination.shape
        buffer = next(ref for ref in buffers if ref.shape[2] == columns and ref.shape[1] >= rows)
        place = buffer.at[slot, pl.ds(0, rows)]
        place[...] = value().astype(BF16)
        copies.append(pltpu.make_async_copy(place, destination, sems.at[slot]))
        copies[-1].start()
    for copy in copies[-SLOTS:]:
        copy.wait()


def weight_kernel(counts, down_experts, *refs):
    normed_chunks, refs = refs[: counts[0]], refs[counts[0] :]
    cot_chunks, refs = refs[: counts[1]], refs[counts[1] :]
    buffers, sems = refs[-3:-1], refs[-1]
    tiles = []
    if counts[0]:
        grads_ref, act_ref = refs[:2]
        gate_out, up_out, down_out, normed, cot = refs[-8:-3]
        assemble(normed, normed_chunks)
        hidden = gate_out.shape[3]
        for e in range(gate_out.shape[1]):
            for i, out in enumerate((gate_out, up_out)):
                first = (2 * e + i) * hidden
                columns = slice(first, first + hidden)
                value = lambda columns=columns: dot(normed[...], grads_ref[:, columns], TN)
                tiles.append((value, out.at[0, e]))
    else:
        act_ref = refs[0]
        down_out, cot = refs[-5:-3]
    assemble(cot, cot_chunks)
    hidden = down_out.shape[2]
    for e in down_experts:
        parts = 2 if e == down_experts[-1] else 1
        step = hidden // parts
        for first in range(0, hidden, step):
            columns = slice(e * hidden + first, e * hidden + first + step)
            value = lambda columns=columns: dot(act_ref[:, columns], cot[...], TN)
            tiles.append((value, down_out.at[0, e, pl.ds(first, step)]))
    write_out(tiles, buffers, sems)


def weight_gradients(cot_chunks, act, down_shape, down_experts, name, started=None, gate_up=None):
    width = cot_chunks[0].shape[1]
    rows = act.shape[0]
    normed_chunks, grads, shapes = gate_up or ([], None, [])
    operands = [*normed_chunks, *cot_chunks, *([grads] if gate_up else []), act]
    specs = [IN_VMEM] * len(operands)
    if started is not None:
        operands, specs = operands + [started], specs + [IN_HBM]
    shapes = [*shapes, down_shape]
    tile = down_shape[2] * width
    flops = 2 * rows * (tile * len(down_experts) + sum(math.prod(shape) for shape in shapes[:-1]))
    slot = (down_shape[2], width)
    return pl.pallas_call(
        functools.partial(weight_kernel, (len(normed_chunks), len(cot_chunks)), down_experts),
        in_specs=specs,
        out_specs=(IN_HBM,) * len(shapes),
        out_shape=tuple(jax.ShapeDtypeStruct(shape, BF16) for shape in shapes),
        input_output_aliases={} if started is None else {len(operands) - 1: len(shapes) - 1},
        scratch_shapes=[pltpu.VMEM((rows, width), BF16)] * (2 if gate_up else 1)
        + [pltpu.VMEM((SLOTS,) + (slot[::-1] if gate_up else (16, 128)), BF16)]
        + [pltpu.VMEM((SLOTS,) + slot, BF16)]
        + [pltpu.SemaphoreType.DMA((SLOTS,))],
        compiler_params=pltpu.CompilerParams(vmem_limit_bytes=24 * MIB),
        cost_estimate=pl.CostEstimate(flops=flops, bytes_accessed=flops // rows, transcendentals=0),
        name=name,
    )(*operands)


def norm_back_kernel(count, *refs):
    parts, (summed_ref, gain_ref, cot_ref) = refs[:count], refs[count : count + 3]
    grad_ref, small_out, *sends = refs[count + 3 :]
    own = summed_ref.shape[0]
    grad_normed = parts[0][:own].astype(F32)
    for part in parts[1:]:
        grad_normed = grad_normed + part[:own].astype(F32)
    summed = summed_ref[...]
    inv_rms = lax.rsqrt(jnp.mean(summed * summed, axis=1, keepdims=True) + 1e-06)
    scaled = grad_normed * gain_ref[...]
    centre = jnp.mean(scaled * summed, axis=1, keepdims=True)
    grad = inv_rms * scaled - summed * (inv_rms * inv_rms * inv_rms * centre)
    grad_ref[...] = grad + cot_ref[...].astype(F32)
    head = sends[0].shape[2]
    for s, send in enumerate(sends):
        place = head_slice(lax.axis_index("tok") ^ (s + 1), head)
        send[0] = grad_ref[:, place].astype(BF16)
    me = lax.axis_index("dp") // 2
    smalls = jnp.stack([one_term(part[own:]) for part in parts])
    small = jnp.zeros(smalls.shape[1:], F32)
    for chip in range(count):
        for i in range(count):
            small = small + jnp.where((me ^ i) == chip, smalls[i], 0.0)
    small_out[...] = small


def norm_backward(parts, summed, gain, cot):
    rows, width = summed.shape
    num_tokens = lax.axis_size("tok")
    head = jax.ShapeDtypeStruct((1, rows, width // num_tokens), BF16)
    return pl.pallas_call(
        functools.partial(norm_back_kernel, len(parts)),
        out_shape=(
            jax.ShapeDtypeStruct((rows, width), F32),
            jax.ShapeDtypeStruct((8, width // 2), F32),
        )
        + (head,) * (num_tokens - 1),
        compiler_params=pltpu.CompilerParams(vmem_limit_bytes=4 * MIB),
        name="norm_backward",
    )(*parts, summed, gain, cot)


def finish_kernel(places, grad_ref, small_ref, other_ref, *refs):
    heads, (out_ref, router_out, gain_out) = refs[:-3], refs[-3:]
    core = lax.axis_index("dp") % 2
    experts, columns = router_out.shape
    for ref, c in ((small_ref, core), (other_ref, 1 - core)):
        place = head_slice(c, columns // 2)
        router_out[:, place] = ref[:experts]
        gain_out[:, place] = ref[experts : experts + 1]
    me = lax.axis_index("tok")
    width = heads[0].shape[2]
    own = head_slice(me, width)
    out_ref[0, :, own] = (2.0 * grad_ref[:, own]).astype(BF16)
    for d, i, j in places:
        place = head_slice(me ^ d, width)
        out_ref[0, :, place] = (grad_ref[:, place] + heads[i][j].astype(F32)).astype(BF16)


def finish(grad_summed, heads, places, small, other, experts):
    rows, width = grad_summed.shape
    return pl.pallas_call(
        functools.partial(finish_kernel, places),
        out_shape=(
            jax.ShapeDtypeStruct((1, rows, width), BF16),
            jax.ShapeDtypeStruct((experts, width), F32),
            jax.ShapeDtypeStruct((1, width), F32),
        ),
        compiler_params=pltpu.CompilerParams(vmem_limit_bytes=4 * MIB),
        name="finish",
    )(grad_summed, small, other, *heads)


def shards(inputs, cotangent, norm_gain, router_weight, route_ids, w_gate, w_up, w_down):
    width = inputs.shape[2]
    size = lax.axis_size("dp")
    experts = w_gate.shape[1]

    x, cot, first, kept = split_heads(inputs, cotangent)
    heads, items = first_stage(first, kept)
    heads, items = other_stages(heads, items)
    cots = gather_chips(cot)
    norm_gain, heads[1] = after((norm_gain, heads[1]))
    gain, router_rows, chosen, down = small_operands(
        norm_gain, router_weight[0].T, route_ids[0].T, w_down
    )
    heads, gain, router_rows, chosen, down = after((heads, gain, router_rows, chosen, down))
    places = from_tokens(heads, items)
    normed, summed = norm_rows(x, gain, heads, places)
    far_rows = gather_chips(normed)
    own_other = exchange(far_rows[0], "dp", 1)
    cots, own_other = after((cots, own_other))
    mine = join_rows(cots)
    w_gate_first, mine = after((w_gate, mine))
    weights = load_first(w_gate_first, w_up)
    other_cots, weights = after((exchange(mine, "dp", 1), weights))
    cots = [mine, other_cots]
    back, weights = back_hidden(cots, down, w_down, w_gate, w_up, weights)
    far_rows[1:], back = after((far_rows[1:], back))
    rows = far_rows + [own_other] + [exchange(chunk, "dp", 1) for chunk in far_rows[1:]]
    grads, act, sent, *kept, small = experts_backward(
        rows, weights, w_gate, w_up, back, chosen, router_rows, gain
    )
    sent, act = after((sent, act))
    arrived = exchange(sent, "dp", 1)
    (grad_down,) = weight_gradients(cots, act, w_down.shape, range(1), "grad_down_0")
    arrived, grad_down, grads = after((arrived, grad_down, grads))
    pairs = pair_sum(kept, arrived, small)
    pairs, grads = after((pairs, grads))
    far = [exchange(pairs[s], "dp", 2 * s) for s in reversed(range(1, size // 2))]
    grad_gate, grad_up, grad_down = weight_gradients(
        cots,
        act,
        w_down.shape,
        range(1, DOWN_MIDDLE),
        "grad_gate_up",
        grad_down,
        (rows, grads, (w_gate.shape, w_up.shape)),
    )
    far, grad_gate, grad_up, grad_down = after((far, grad_gate, grad_up, grad_down))
    grad_summed, small, *sends = norm_backward([pairs[0]] + far[::-1], summed, gain, cot)
    sends, act, small = after((sends, act, small))
    other = exchange(small, "dp", 1)
    returned = [exchange(send, "tok", s + 1) for s, send in reversed(list(enumerate(sends)))]
    (grad_down,) = weight_gradients(
        cots, act, w_down.shape, range(DOWN_MIDDLE, experts), "grad_down", grad_down
    )
    returned, grad_down, other = after((returned, grad_down, other))
    places = tuple((len(returned) - s, s, 0) for s in range(len(returned)))
    grad_inputs, grad_router, grad_gain = finish(grad_summed, returned, places, small, other, experts)
    return (
        grad_inputs,
        grad_gate,
        grad_up,
        grad_down,
        grad_router.T[None],
        grad_gain,
    )


def solution(mesh):
    return jax.shard_map(
        shards,
        mesh=mesh,
        in_specs=(
            P("tok", "dp", None),
            P("tok", "dp", None),
            P("tok", None),
            P("tok", None, None),
            P("tok", None, None),
            P("tok", None, None, "dp"),
            P("tok", None, None, "dp"),
            P("tok", None, "dp", None),
        ),
        out_specs=(
            P("tok", "dp", None),
            P("tok", None, None, "dp"),
            P("tok", None, None, "dp"),
            P("tok", None, "dp", None),
            P("tok", None, None),
            P("tok", None),
        ),
        check_vma=False,
    )
```

```python
import functools
import math

import jax
import jax.numpy as jnp
from jax import lax
from jax.experimental import pallas as pl
from jax.experimental.pallas import tpu as pltpu
from jax.sharding import PartitionSpec as P

BF16 = jnp.bfloat16
F32 = jnp.float32
MIB = 1024 * 1024


def dot(left, right, dims):
    return lax.dot_general(left, right, (dims, ((), ())), preferred_element_type=F32)


NN = ((1,), (0,))
NT = ((1,), (1,))
TN = ((0,), (0,))


def exchange(value, axis, distance):
    size = lax.axis_size(axis)
    return lax.ppermute(value, axis, [(i, i ^ distance) for i in range(size)])


def gather_chips(rows):
    size = lax.axis_size("dp")
    return [rows] + [exchange(rows, "dp", s) for s in range(2, size, 2)]


def gather_cores(chunks):
    return list(chunks) + [exchange(chunk, "dp", 1) for chunk in chunks]


def after(values):
    return lax.optimization_barrier(values)


def device_of(block, size):
    return 2 * block if block < size // 2 else 2 * block + 1 - size


def assemble(rows, chunks):
    first = 0
    for chunk in chunks:
        rows[first : first + chunk.shape[0]] = chunk[...]
        first += chunk.shape[0]


def head_slice(slot, width):
    return pl.ds(pl.multiple_of(slot * width, width), width)


def hbm(array):
    return pltpu.with_memory_space_constraint(array, pltpu.HBM)


def vmem(array):
    return pltpu.with_memory_space_constraint(array, pltpu.VMEM)


IN_HBM = pl.BlockSpec(memory_space=pltpu.HBM)
IN_VMEM = pl.BlockSpec(memory_space=pltpu.VMEM)
ANYWHERE = pl.BlockSpec(memory_space=pl.ANY)


def head_plan(num_tokens):
    held, stages, bit = [(0, d) for d in range(1, num_tokens)], [], 1
    while bit < num_tokens:
        sent = [item for item in held if item[1] & bit]
        received = [(source ^ bit, target ^ bit) for source, target in sent]
        held = [item for item in held if not item[1] & bit] + received
        stages.append((bit, sent, received))
        bit *= 2
    first = stages[0][1]
    return first, [(0, d) for d in range(1, num_tokens) if (0, d) not in first], stages


def pick(item, lists):
    for i, items in enumerate(lists):
        if item in items:
            return i, items.index(item)


def pack_kernel(picks, *refs):
    for k, (i, j) in enumerate(picks):
        refs[-1][k] = refs[i][j]


def pack_heads(arrays, picks):
    return pl.pallas_call(
        functools.partial(pack_kernel, picks),
        out_shape=jax.ShapeDtypeStruct((len(picks),) + arrays[0].shape[1:], BF16),
        compiler_params=pltpu.CompilerParams(vmem_limit_bytes=4 * MIB),
        name="pack_heads",
    )(*arrays)


def first_stage(first, kept):
    _, kept_items, stages = head_plan(lax.axis_size("tok"))
    bit, _, received = stages[0]
    return [kept, exchange(first, "tok", bit)], [kept_items, received]


def other_stages(arrays, lists):
    for bit, sent, received in head_plan(lax.axis_size("tok"))[2][1:]:
        payload = pack_heads(arrays, [pick(item, lists) for item in sent])
        arrays = arrays + [exchange(payload, "tok", bit)]
        lists = lists + [received]
    return arrays, lists


def heads_kernel(x_hbm, cot_hbm, x_ref, cot_ref, first_ref, kept_ref, sems):
    copy_x = pltpu.make_async_copy(x_hbm.at[0], x_ref, sems.at[0])
    copy_cot = pltpu.make_async_copy(cot_hbm.at[0], cot_ref, sems.at[1])
    copy_x.start()
    copy_cot.start()
    copy_x.wait()
    store_heads(x_ref, first_ref, kept_ref)
    copy_cot.wait()


def store_heads(rows_ref, first_ref, kept_ref):
    width = first_ref.shape[2]
    first, kept, _ = head_plan(rows_ref.shape[1] // width)
    me = lax.axis_index("tok")
    for ref, items in ((first_ref, first), (kept_ref, kept)):
        for k, (_, d) in enumerate(items):
            ref[k] = rows_ref[:, head_slice(me ^ d, width)].astype(BF16)


def head_shapes(rows, width):
    num_tokens = lax.axis_size("tok")
    first, kept, _ = head_plan(num_tokens)
    return tuple(
        jax.ShapeDtypeStruct((len(items), rows, width // num_tokens), BF16) for items in (first, kept)
    )


def split_heads(x, cotangent):
    _, rows, width = x.shape
    return pl.pallas_call(
        heads_kernel,
        in_specs=[IN_HBM] * 2,
        out_shape=(jax.ShapeDtypeStruct((rows, width), BF16),) * 2 + head_shapes(rows, width),
        scratch_shapes=[pltpu.SemaphoreType.DMA((2,))],
        compiler_params=pltpu.CompilerParams(vmem_limit_bytes=4 * MIB),
        name="split_heads",
    )(hbm(x), hbm(cotangent))


def from_tokens(arrays, lists):
    num_tokens = lax.axis_size("tok")
    return tuple((d,) + pick((d, 0), lists) for d in range(1, num_tokens))


def small_kernel(gain_hbm, router_in, route_hbm, down_hbm, *refs):
    gain_ref, router_ref, chosen_ref, down_ref, routes, sems, down_sem = refs
    load = pltpu.make_async_copy(down_hbm.at[0, pl.ds(0, down_ref.shape[0])], down_ref, down_sem)
    load.start()
    copies = [
        pltpu.make_async_copy(src, dst, sems.at[i])
        for i, (src, dst) in enumerate(
            [
                (gain_hbm, gain_ref),
                (route_hbm, routes),
            ]
        )
    ]
    for copy in copies:
        copy.start()
    router_ref[...] = router_in[...]
    for copy in copies:
        copy.wait()
    rows, experts = chosen_ref.shape
    ids = lax.broadcasted_iota(jnp.int32, (experts, rows), 0)
    hit = routes[0:1, :] == ids
    for k in range(1, routes.shape[0]):
        hit = hit | (routes[k : k + 1, :] == ids)
    chosen_ref[...] = hit.astype(F32).T
    load.wait()


def small_operands(gain, router_rows, routes, w_down):
    experts, all_rows = 8, routes.shape[1]
    return pl.pallas_call(
        small_kernel,
        in_specs=[IN_HBM, IN_VMEM, IN_HBM, IN_HBM],
        out_specs=(IN_VMEM,) * 3 + (ANYWHERE,),
        out_shape=(
            jax.ShapeDtypeStruct(gain.shape, F32),
            jax.ShapeDtypeStruct(router_rows.shape, BF16),
            jax.ShapeDtypeStruct((all_rows, experts), F32),
            jax.ShapeDtypeStruct((w_down.shape[1] - 1,) + w_down.shape[2:], BF16),
        ),
        scratch_shapes=[
            pltpu.VMEM(routes.shape, jnp.int32),
            pltpu.SemaphoreType.DMA((2,)),
            pltpu.SemaphoreType.DMA(()),
        ],
        compiler_params=pltpu.CompilerParams(vmem_limit_bytes=4 * MIB),
        cost_estimate=pl.CostEstimate(flops=2**36, bytes_accessed=32 * MIB, transcendentals=0),
        name="small_operands",
    )(hbm(gain), router_rows, hbm(routes), hbm(w_down))


def norm_kernel(places, x_ref, gain_ref, *refs):
    heads, (normed_ref, summed_ref) = refs[:-2], refs[-2:]
    me = lax.axis_index("tok")
    width = heads[0].shape[2]
    own = head_slice(me, width)
    summed_ref[:, own] = 2.0 * x_ref[:, own].astype(F32)
    for d, i, j in places:
        place = head_slice(me ^ d, width)
        summed_ref[:, place] = x_ref[:, place].astype(F32) + heads[i][j].astype(F32)
    summed = summed_ref[...]
    inv_rms = lax.rsqrt(jnp.mean(summed * summed, axis=1, keepdims=True) + 1e-06)
    normed_ref[...] = (summed * inv_rms * gain_ref[...]).astype(BF16)


def norm_rows(x, gain, heads, places):
    return pl.pallas_call(
        functools.partial(norm_kernel, places),
        out_shape=(jax.ShapeDtypeStruct(x.shape, BF16), jax.ShapeDtypeStruct(x.shape, F32)),
        compiler_params=pltpu.CompilerParams(vmem_limit_bytes=4 * MIB),
        name="norm_rows",
    )(x, gain, *heads)


def join_kernel(*refs):
    assemble(refs[-1], refs[:-1])


def join_rows(chunks):
    rows, width = sum(chunk.shape[0] for chunk in chunks), chunks[0].shape[1]
    return pl.pallas_call(
        join_kernel,
        out_shape=jax.ShapeDtypeStruct((rows, width), BF16),
        compiler_params=pltpu.CompilerParams(vmem_limit_bytes=4 * MIB),
        name="join_rows",
    )(*chunks)


def load_weights(refs, place, experts, sems, start=0):
    copies = []
    for i, (e, ref) in enumerate((e, ref) for e in experts for ref in refs):
        hidden = ref.shape[3]
        columns = pl.ds((2 * start + i) * hidden, hidden)
        copies.append(pltpu.make_async_copy(ref.at[0, e], place.at[:, columns], sems.at[i]))
        copies[-1].start()
    return copies


def load_kernel(gate_hbm, up_hbm, weights_ref, sems):
    for load in load_weights((gate_hbm, up_hbm), weights_ref, range(1), sems):
        load.wait()


def load_first(w_gate, w_up):
    _, experts, width, hidden = w_gate.shape
    return pl.pallas_call(
        load_kernel,
        in_specs=[IN_HBM] * 2,
        out_specs=ANYWHERE,
        out_shape=jax.ShapeDtypeStruct((width, experts // 2 * 2 * hidden), BF16),
        scratch_shapes=[pltpu.SemaphoreType.DMA((2,))],
        compiler_params=pltpu.CompilerParams(vmem_limit_bytes=1 * MIB),
        cost_estimate=pl.CostEstimate(flops=2**36, bytes_accessed=4 * width * hidden, transcendentals=0),
        name="load_first",
    )(hbm(w_gate), hbm(w_up))


def back_kernel(count, *refs):
    chunks, (first, down_hbm, gate_hbm, up_hbm, _, back_ref, weights_ref) = refs[:count], refs[count : count + 7]
    cot, second, down_sems, sems = refs[count + 7 :]
    split = first.shape[0]
    experts = split + second.shape[0]
    copies = [
        pltpu.make_async_copy(down_hbm.at[0, split + e], second.at[e], down_sems.at[e])
        for e in range(experts - split)
    ]
    for copy in copies:
        copy.start()
    loads = load_weights((gate_hbm, up_hbm), weights_ref, range(1, experts // 2), sems, 1)
    assemble(cot, chunks)
    for e in range(split):
        back_ref[e] = dot(cot[...], first[e], NT)
    for e, copy in enumerate(copies):
        copy.wait()
        back_ref[split + e] = dot(cot[...], second[e], NT)
    for load in loads:
        load.wait()


def back_hidden(chunks, first, w_down, w_gate, w_up, weights):
    _, experts, hidden, width = w_down.shape
    rows = sum(chunk.shape[0] for chunk in chunks)
    rest = experts - first.shape[0]
    return pl.pallas_call(
        functools.partial(back_kernel, len(chunks)),
        in_specs=[IN_VMEM] * (len(chunks) + 1) + [IN_HBM] * 3 + [ANYWHERE],
        input_output_aliases={len(chunks) + 4: 1},
        out_specs=(IN_VMEM, ANYWHERE),
        out_shape=(
            jax.ShapeDtypeStruct((experts, rows, hidden), F32),
            jax.ShapeDtypeStruct((width, experts // 2 * 2 * hidden), BF16),
        ),
        scratch_shapes=[
            pltpu.VMEM((rows, width), BF16),
            pltpu.VMEM((rest, hidden, width), BF16),
            pltpu.SemaphoreType.DMA((rest,)),
            pltpu.SemaphoreType.DMA(((experts // 2 - 1) * 2,)),
        ],
        compiler_params=pltpu.CompilerParams(vmem_limit_bytes=16 * MIB),
        cost_estimate=pl.CostEstimate(
            flops=0,
            bytes_accessed=0,
            transcendentals=0,
        ),
        name="back_hidden",
    )(*chunks, vmem(first), hbm(w_down), hbm(w_gate), hbm(w_up), weights)


def expert_kernel(size, *refs):
    chunks, (first, gate_hbm, up_hbm, back_ref) = refs[:size], refs[size : size + 4]
    chosen_ref, router_ref, gain_ref, grads_out, act_out, sent_out = refs[size + 4 : size + 10]
    kept, (small_out, normed, total, second, sems) = refs[size + 10 : -5], refs[-5:]
    own, width = chunks[0].shape
    experts = router_ref.shape[0]
    hidden = back_ref.shape[2]
    split = experts // 2
    loads = load_weights((gate_hbm, up_hbm), second, range(split, experts), sems)
    assemble(normed, chunks)
    me = lax.axis_index("dp")
    hits = []
    for i in range(size):
        start = pl.multiple_of((me ^ device_of(i, size)) * own, own)
        hits.append(chosen_ref[pl.ds(start, own), :experts])
    chosen = jnp.concatenate(hits, axis=0)
    prob = jax.nn.sigmoid(dot(normed[...], router_ref[...], NT))
    gates = prob * chosen

    def forward(e):
        if e < split:
            return dot(normed[...], first[:, 2 * e * hidden : 2 * (e + 1) * hidden], NN)
        e -= split
        loads[2 * e].wait()
        loads[2 * e + 1].wait()
        return dot(normed[...], second[:, 2 * e * hidden : 2 * (e + 1) * hidden], NN)

    shares = []
    later = forward(0)
    for e in range(experts):
        pre_gate, pre_up = later[:, :hidden], later[:, hidden:]
        if e + 1 < experts:
            later = forward(e + 1)
        gate = gates[:, e : e + 1]
        back = back_ref[e]
        sigma = jax.nn.sigmoid(pre_gate)
        silu = pre_gate * sigma
        act = silu * pre_up
        shares.append(jnp.sum(act * back, axis=1, keepdims=True))
        scaled = gate * back
        grad_gate = scaled * pre_up * (sigma * (1.0 + pre_gate * (1.0 - sigma)))
        grads_out[:, 2 * e * hidden : (2 * e + 1) * hidden] = grad_gate.astype(BF16)
        grads_out[:, (2 * e + 1) * hidden : (2 * e + 2) * hidden] = (scaled * silu).astype(BF16)
        act_out[:, e * hidden : (e + 1) * hidden] = (gate * act).astype(BF16)
        if e == experts - 2:
            total[...] = dot(grads_out[:, : 2 * split * hidden], first[...], NT)
    coef = jnp.concatenate(shares, axis=1) * gates * (1.0 - prob)
    high = coef.astype(BF16).astype(F32)
    middle = (coef - high).astype(BF16).astype(F32)
    low = coef - high - middle
    terms = jnp.concatenate([high, middle, low], axis=1).astype(BF16)
    router = router_ref[...].astype(F32)
    router = jnp.concatenate([router] * 3, axis=0).astype(BF16)
    small = dot(terms, normed[...], TN)
    small_out[:experts] = small[:experts] + small[experts : 2 * experts] + small[2 * experts :]
    half = size // 2 * own
    step = width // 4
    for c in range(0, width, step):
        here = slice(c, c + step)
        grad = total[:, here] + dot(grads_out[:, 2 * split * hidden :], second[here, :], NT)
        grad = grad + dot(terms, router[:, here], NN)
        rows_here = normed[:, here].astype(F32)
        gain = jnp.sum(grad * rows_here, axis=0, keepdims=True) / gain_ref[:, here]
        small_out[experts:, here] = jnp.broadcast_to(gain, (8 - experts, step))
        grad = grad.astype(BF16)
        for i in range(size // 2):
            kept[i][:, here] = grad[i * own : (i + 1) * own]
        sent_out[:half, here] = grad[half:]
    sent_out[half:] = wide_terms(small_out[...])


def experts_backward(chunks, first, w_gate, w_up, back, chosen, router_rows, gain):
    size = len(chunks)
    own, width = chunks[0].shape
    experts, rows, hidden = back.shape
    kept = jax.ShapeDtypeStruct((own, width), BF16)
    return pl.pallas_call(
        functools.partial(expert_kernel, size),
        in_specs=[IN_VMEM] * (size + 1) + [IN_HBM] * 2 + [IN_VMEM] * 4,
        out_shape=(
            jax.ShapeDtypeStruct((rows, 2 * experts * hidden), BF16),
            jax.ShapeDtypeStruct((rows, experts * hidden), BF16),
            jax.ShapeDtypeStruct((rows // 2 + 16, width), BF16),
        )
        + (kept,) * (size // 2)
        + (jax.ShapeDtypeStruct((8, width), F32),),
        scratch_shapes=[
            pltpu.VMEM((rows, width), BF16),
            pltpu.VMEM((rows, width), F32),
            pltpu.VMEM((width, 2 * (experts - experts // 2) * hidden), BF16),
            pltpu.SemaphoreType.DMA((2 * (experts - experts // 2),)),
        ],
        compiler_params=pltpu.CompilerParams(vmem_limit_bytes=20 * MIB),
        cost_estimate=pl.CostEstimate(
            flops=8 * experts * rows * hidden * width,
            bytes_accessed=experts * hidden * (width * 4 + rows * 10) + rows * width * 4,
            transcendentals=experts * rows * hidden,
        ),
        name="experts_backward",
    )(*chunks, vmem(first), hbm(w_gate), hbm(w_up), back, chosen, router_rows, gain)


def two_terms(small):
    high = small.astype(BF16).astype(F32)
    return high, small - high


def wide_terms(small):
    return jnp.concatenate(two_terms(small), axis=0).astype(BF16)


def tall_terms(small):
    half = small.shape[1] // 2
    terms = [term[:, c : c + half] for c in (0, half) for term in two_terms(small)]
    return jnp.concatenate(terms, axis=0).astype(BF16)


def from_tall(terms):
    terms = terms.astype(F32)
    return jnp.concatenate([terms[:8] + terms[8:16], terms[16:24] + terms[24:32]], axis=1)


def pair_kernel(count, *refs):
    kept, (arrived_ref, small_ref) = refs[:count], refs[count : count + 2]
    outs, total_ref = refs[count + 2 : -1], refs[-1]
    own, width = kept[0].shape
    core = lax.axis_index("dp") % 2
    arrived = arrived_ref[count * own :].astype(F32)
    total_ref[...] = small_ref[...] + arrived[:8] + arrived[8:]
    small = tall_terms(total_ref[:, head_slice(core, width // 2)])
    for i in range(count):
        arrived = arrived_ref[i * own : (i + 1) * own].astype(F32)
        outs[i][:, :width] = (kept[i][...].astype(F32) + arrived).astype(BF16)
        outs[i][:32, width:] = small
        if own > 32:
            outs[i][32:, width:] = jnp.zeros((own - 32, width // 4), BF16)


def pair_sum(kept, arrived, small):
    own, width = kept[0].shape
    return pl.pallas_call(
        functools.partial(pair_kernel, len(kept)),
        out_shape=(jax.ShapeDtypeStruct((own, width + width // 4), BF16),) * len(kept),
        scratch_shapes=[pltpu.VMEM(small.shape, F32)],
        compiler_params=pltpu.CompilerParams(vmem_limit_bytes=4 * MIB),
        name="pair_sum",
    )(*kept, arrived, small)


SLOTS = 4
DOWN_MIDDLE = 2


def write_out(tiles, buffers, sems):
    copies = []
    for i, (value, destination) in enumerate(tiles):
        slot = i % SLOTS
        if i >= SLOTS:
            copies[i - SLOTS].wait()
        rows, columns = destination.shape
        buffer = next(ref for ref in buffers if ref.shape[2] == columns and ref.shape[1] >= rows)
        place = buffer.at[slot, pl.ds(0, rows)]
        place[...] = value().astype(BF16)
        copies.append(pltpu.make_async_copy(place, destination, sems.at[slot]))
        copies[-1].start()
    for copy in copies[-SLOTS:]:
        copy.wait()


def weight_kernel(counts, down_experts, *refs):
    normed_chunks, refs = refs[: counts[0]], refs[counts[0] :]
    cot_chunks, refs = refs[: counts[1]], refs[counts[1] :]
    buffers, sems = refs[-3:-1], refs[-1]
    tiles = []
    if counts[0]:
        grads_ref, act_ref = refs[:2]
        gate_out, up_out, down_out, normed, cot = refs[-8:-3]
        assemble(normed, normed_chunks)
        hidden = gate_out.shape[3]
        for e in range(gate_out.shape[1]):
            for i, out in enumerate((gate_out, up_out)):
                first = (2 * e + i) * hidden
                columns = slice(first, first + hidden)
                value = lambda columns=columns: dot(normed[...], grads_ref[:, columns], TN)
                tiles.append((value, out.at[0, e]))
    else:
        act_ref = refs[0]
        down_out, cot = refs[-5:-3]
    assemble(cot, cot_chunks)
    hidden = down_out.shape[2]
    for e in down_experts:
        parts = 2
        step = hidden // parts
        for first in range(0, hidden, step):
            columns = slice(e * hidden + first, e * hidden + first + step)
            value = lambda columns=columns: dot(act_ref[:, columns], cot[...], TN)
            tiles.append((value, down_out.at[0, e, pl.ds(first, step)]))
    write_out(tiles, buffers, sems)


def weight_gradients(cot_chunks, act, down_shape, down_experts, name, started=None, gate_up=None):
    width = cot_chunks[0].shape[1]
    rows = act.shape[0]
    normed_chunks, grads, shapes = gate_up or ([], None, [])
    operands = [*normed_chunks, *cot_chunks, *([grads] if gate_up else []), act]
    specs = [IN_VMEM] * len(operands)
    if started is not None:
        operands, specs = operands + [started], specs + [IN_HBM]
    shapes = [*shapes, down_shape]
    tile = down_shape[2] * width
    flops = 2 * rows * (tile * len(down_experts) + sum(math.prod(shape) for shape in shapes[:-1]))
    slot = (down_shape[2], width)
    return pl.pallas_call(
        functools.partial(weight_kernel, (len(normed_chunks), len(cot_chunks)), down_experts),
        in_specs=specs,
        out_specs=(IN_HBM,) * len(shapes),
        out_shape=tuple(jax.ShapeDtypeStruct(shape, BF16) for shape in shapes),
        input_output_aliases={} if started is None else {len(operands) - 1: len(shapes) - 1},
        scratch_shapes=[pltpu.VMEM((rows, width), BF16)] * (2 if gate_up else 1)
        + [pltpu.VMEM((SLOTS,) + (slot[::-1] if gate_up else (16, 128)), BF16)]
        + [pltpu.VMEM((SLOTS,) + slot, BF16)]
        + [pltpu.SemaphoreType.DMA((SLOTS,))],
        compiler_params=pltpu.CompilerParams(vmem_limit_bytes=24 * MIB),
        cost_estimate=pl.CostEstimate(flops=flops, bytes_accessed=flops // rows, transcendentals=0),
        name=name,
    )(*operands)


def norm_back_kernel(count, *refs):
    parts, (summed_ref, gain_ref, cot_ref) = refs[:count], refs[count : count + 3]
    grad_ref, small_out, *sends = refs[count + 3 :]
    full = summed_ref.shape[1]
    grad_normed = parts[0][:, :full].astype(F32)
    for part in parts[1:]:
        grad_normed = grad_normed + part[:, :full].astype(F32)
    summed = summed_ref[...]
    inv_rms = lax.rsqrt(jnp.mean(summed * summed, axis=1, keepdims=True) + 1e-06)
    scaled = grad_normed * gain_ref[...]
    centre = jnp.mean(scaled * summed, axis=1, keepdims=True)
    grad = inv_rms * scaled - summed * (inv_rms * inv_rms * inv_rms * centre)
    grad_ref[...] = grad + cot_ref[...].astype(F32)
    head = sends[0].shape[2]
    for s, send in enumerate(sends):
        place = head_slice(lax.axis_index("tok") ^ (s + 1), head)
        send[0] = grad_ref[:, place].astype(BF16)
    me = lax.axis_index("dp") // 2
    smalls = jnp.stack([from_tall(part[:32, full:]) for part in parts])
    small = jnp.zeros(smalls.shape[1:], F32)
    for chip in range(count):
        for i in range(count):
            small = small + jnp.where((me ^ i) == chip, smalls[i], 0.0)
    small_out[...] = small


def norm_backward(parts, summed, gain, cot):
    rows, width = summed.shape
    num_tokens = lax.axis_size("tok")
    head = jax.ShapeDtypeStruct((1, rows, width // num_tokens), BF16)
    return pl.pallas_call(
        functools.partial(norm_back_kernel, len(parts)),
        out_shape=(
            jax.ShapeDtypeStruct((rows, width), F32),
            jax.ShapeDtypeStruct((8, width // 2), F32),
        )
        + (head,) * (num_tokens - 1),
        compiler_params=pltpu.CompilerParams(vmem_limit_bytes=4 * MIB),
        name="norm_backward",
    )(*parts, summed, gain, cot)


def finish_kernel(places, grad_ref, small_ref, other_ref, *refs):
    heads, (out_ref, router_out, gain_out) = refs[:-3], refs[-3:]
    core = lax.axis_index("dp") % 2
    experts, columns = router_out.shape
    for ref, c in ((small_ref, core), (other_ref, 1 - core)):
        place = head_slice(c, columns // 2)
        router_out[:, place] = ref[:experts]
        gain_out[:, place] = ref[experts : experts + 1]
    me = lax.axis_index("tok")
    width = heads[0].shape[2]
    own = head_slice(me, width)
    out_ref[0, :, own] = (2.0 * grad_ref[:, own]).astype(BF16)
    for d, i, j in places:
        place = head_slice(me ^ d, width)
        out_ref[0, :, place] = (grad_ref[:, place] + heads[i][j].astype(F32)).astype(BF16)


def finish(grad_summed, heads, places, small, other, experts):
    rows, width = grad_summed.shape
    return pl.pallas_call(
        functools.partial(finish_kernel, places),
        out_shape=(
            jax.ShapeDtypeStruct((1, rows, width), BF16),
            jax.ShapeDtypeStruct((experts, width), F32),
            jax.ShapeDtypeStruct((1, width), F32),
        ),
        compiler_params=pltpu.CompilerParams(vmem_limit_bytes=4 * MIB),
        name="finish",
    )(grad_summed, small, other, *heads)


def shards(inputs, cotangent, norm_gain, router_weight, route_ids, w_gate, w_up, w_down):
    width = inputs.shape[2]
    size = lax.axis_size("dp")
    experts = w_gate.shape[1]

    x, cot, first, kept = split_heads(inputs, cotangent)
    heads, items = first_stage(first, kept)
    heads, items = other_stages(heads, items)
    cots = gather_chips(cot)
    norm_gain, heads[1] = after((norm_gain, heads[1]))
    gain, router_rows, chosen, down = small_operands(
        norm_gain, router_weight[0].T, route_ids[0].T, w_down
    )
    heads, gain, router_rows, chosen, down = after((heads, gain, router_rows, chosen, down))
    places = from_tokens(heads, items)
    normed, summed = norm_rows(x, gain, heads, places)
    far_rows = gather_chips(normed)
    own_other = exchange(far_rows[0], "dp", 1)
    cots, own_other = after((cots, own_other))
    mine = join_rows(cots)
    w_gate_first, mine = after((w_gate, mine))
    weights = load_first(w_gate_first, w_up)
    other_cots, weights = after((exchange(mine, "dp", 1), weights))
    cots = [mine, other_cots]
    back, weights = back_hidden(cots, down, w_down, w_gate, w_up, weights)
    far_rows[1:], back = after((far_rows[1:], back))
    rows = far_rows + [own_other] + [exchange(chunk, "dp", 1) for chunk in far_rows[1:]]
    grads, act, sent, *kept, small = experts_backward(
        rows, weights, w_gate, w_up, back, chosen, router_rows, gain
    )
    sent, act = after((sent, act))
    arrived = exchange(sent, "dp", 1)
    (grad_down,) = weight_gradients(cots, act, w_down.shape, range(1), "grad_down_0")
    arrived, grad_down, grads = after((arrived, grad_down, grads))
    pairs = pair_sum(kept, arrived, small)
    pairs, grads = after((pairs, grads))
    far = [exchange(pairs[s], "dp", 2 * s) for s in reversed(range(1, size // 2))]
    grad_gate, grad_up, grad_down = weight_gradients(
        cots,
        act,
        w_down.shape,
        range(1, DOWN_MIDDLE),
        "grad_gate_up",
        grad_down,
        (rows, grads, (w_gate.shape, w_up.shape)),
    )
    far, grad_gate, grad_up, grad_down = after((far, grad_gate, grad_up, grad_down))
    grad_summed, small, *sends = norm_backward([pairs[0]] + far[::-1], summed, gain, cot)
    sends, act, small = after((sends, act, small))
    other = exchange(small, "dp", 1)
    returned = [exchange(send, "tok", s + 1) for s, send in reversed(list(enumerate(sends)))]
    (grad_down,) = weight_gradients(
        cots, act, w_down.shape, range(DOWN_MIDDLE, experts), "grad_down", grad_down
    )
    returned, grad_down, other = after((returned, grad_down, other))
    places = tuple((len(returned) - s, s, 0) for s in range(len(returned)))
    grad_inputs, grad_router, grad_gain = finish(grad_summed, returned, places, small, other, experts)
    return (
        grad_inputs,
        grad_gate,
        grad_up,
        grad_down,
        grad_router.T[None],
        grad_gain,
    )


def solution(mesh):
    return jax.shard_map(
        shards,
        mesh=mesh,
        in_specs=(
            P("tok", "dp", None),
            P("tok", "dp", None),
            P("tok", None),
            P("tok", None, None),
            P("tok", None, None),
            P("tok", None, None, "dp"),
            P("tok", None, None, "dp"),
            P("tok", None, "dp", None),
        ),
        out_specs=(
            P("tok", "dp", None),
            P("tok", None, None, "dp"),
            P("tok", None, None, "dp"),
            P("tok", None, "dp", None),
            P("tok", None, None),
            P("tok", None),
        ),
        check_vma=False,
    )
```
